256 devices in a mesh: segment: 2 (over x_lo), blk: 32 (over z, x_hi, core), mp: 4 (over y).
Axes of the slice: x: 4 (x_hi: 2, x_lo: 2; x = x_hi * 2 + x_lo), y: 4, z: 8, core: 2. Of those that a mesh axis runs over, the one named last changes fastest.
Arguments:
- segment_in: bfloat16 [2, 8192, 4096], P('segment', 'blk'), may hold values from -7.5 to 7.5
- norm_gains: float32 [2, 4096], P('segment'), may hold values from 0.25 to 1.75
- projections: bfloat16 [2, 4096, 2, 2048], P('segment', None, None, 'mp'), may hold values from -2 to 2
- live_counts: int32 [2, 32], P(None, 'blk'), may hold values from 1 to 256, 6144 in all within a row
- cotangent: bfloat16 [8192, 4096], P('blk', 'mp'), may hold values from -6 to 6
Outputs:
- segment_out: bfloat16 [2, 8192, 4096], P('segment', 'blk', 'mp')
- state_grads: bfloat16 [2, 8192, 4096], P('segment', 'blk', 'mp')
The draws below stay inside these ranges and needn't reach their ends.
Inputs may be any that keep to these rules, and one draw needn't show every extreme that they name: `live_counts`: each row sums to 6144; every entry is at least 1; each row has an entry equal to 256.
All inputs are finite; a program needn't handle non-finite values. No bound on the sum of `live_counts` on one device may be relied on, other than what follows from the above.
Results may differ from the reference program's by a relative error of at most 0.015.
Values may be sent and summed in bfloat16 or wider, within the bound.
A program may use at most 128 MiB of HBM per device.

```python
import math
import jax
import jax.numpy as jnp
import numpy as np
from jax import lax

D = 4096
H = 32
DH = 64
B = 256
WIN = 4
C = 2048
ROWS = 8192
N_BLK = 32
N_MP = 4


def draw_segment_in(key, part):
    base = jax.random.fold_in(key, 7002)
    noise_key = jax.random.fold_in(base, 0)
    noise = jnp.clip(jax.random.normal(noise_key, (2, ROWS, D), jnp.float32), -6.0, 6.0)
    return noise.astype(jnp.bfloat16)


def draw_projections(key, part):
    base = jax.random.fold_in(key, 7003)
    weights = jnp.clip(jax.random.normal(base, (2, D, 2, C), jnp.float32), -6.0, 6.0) / jnp.sqrt(jnp.float32(D))
    return weights.astype(jnp.bfloat16)


def steps_of(own_key, extent, cuts, smallest, top_value):
    def one(axis_at, shards_of):
        steps = jax.random.uniform(jax.random.fold_in(jax.random.fold_in(own_key, 6), axis_at), (shards_of,), jnp.float32, smallest / len(cuts), top_value / len(cuts))
        return jnp.repeat(jnp.exp(steps), extent[axis_at] // shards_of).reshape((-1,) + (1,) * (len(extent) - axis_at - 1))

    loudness = one(*cuts[0])
    for cut in cuts[1:]:
        loudness = loudness * one(*cut)
    return loudness


def length_profile(amount, total, most, skew):
    portions = [(1 << 20) // math.isqrt(grade ** skew) + 1 for grade in range(2, amount + 1)]
    rest, counts = total - most - (amount - 1), [1] * (amount - 1)
    while rest > 0:
        free = [i for i in range(amount - 1) if counts[i] < most]
        mass, budget = sum([portions[i] for i in free]), rest
        for i in free:
            extra = min(most - counts[i], max(1, budget * portions[i] // mass), rest)
            counts[i] = counts[i] + extra
            rest = rest - extra
    return np.array([most] + counts)


def ragged(stream_key, amount, total, bound, slope):
    if amount == 2:
        one = jax.random.randint(stream_key, (), max(1, total - bound), min(bound, total - 1) + 1)
        return jnp.stack([one, total - one])
    sizes = jnp.asarray(length_profile(amount, total, bound, slope), jnp.int32)
    couples = (amount - 1) // 2
    source_of, receiver = sizes[1:1 + 2 * couples:2], sizes[2:2 + 2 * couples:2]
    room = jnp.minimum(source_of - 1, bound - receiver)
    passed = jax.random.randint(jax.random.fold_in(stream_key, 1), (couples,), 0, 1 << 20) % (room + 1)
    sizes = sizes.at[1:1 + 2 * couples:2].set(source_of - passed).at[2:2 + 2 * couples:2].set(receiver + passed)
    return sizes[jax.random.permutation(jax.random.fold_in(stream_key, 2), amount)]


def centred(stream_key, dims, scale, bound, cuts=(), held_as=jnp.bfloat16):
    array = jax.random.normal(stream_key, dims, jnp.float32) * scale
    if len(cuts) > 0:
        array = steps_of(stream_key, dims, cuts, -0.22, 0.18) * array
    return jnp.clip(array, min=-bound, max=bound).astype(held_as)


def setup_inputs(seed: int = 0) -> dict:
    seeds = jax.random.split(jax.random.key(seed), 6)
    segment_in = draw_segment_in(jax.random.fold_in(seeds[5], 71), 0)
    norm_gains = jnp.clip(1.0 + 0.15 * jax.random.normal(seeds[1], (2, D), jnp.float32), 0.25, 1.75)
    projections = draw_projections(jax.random.fold_in(seeds[5], 71), 0)
    live_counts = jax.vmap(lambda own: ragged(own, N_BLK, N_BLK * B * 3 // 4, B, 0))(jax.random.split(seeds[3], 2)).reshape((2, N_BLK)).astype(jnp.int32)
    cotangent = centred(seeds[4], (ROWS, D), 1.0, 6.0, ((0, 32), (1, 4)))
    return dict(segment_in=segment_in, norm_gains=norm_gains, projections=projections, live_counts=live_counts, cotangent=cotangent)


EPSILON = 1e-06
SCALE = 0.125
NEGATIVE = -1e+30

def normalize(states, gain_row):
    widened = states.astype(jnp.float32)
    spread = jnp.sqrt(lax.optimization_barrier(jnp.mean(widened * widened, axis=-1, keepdims=True)) + EPSILON)
    return ((widened / spread * gain_row).astype(jnp.bfloat16), spread)

def grouped_product(pairs):
    group_width = pairs[0][0].shape[1] // N_MP
    total = jnp.zeros((pairs[0][0].shape[0], pairs[0][1].shape[0]), jnp.float32)
    for group in range(N_MP):
        lower = group * group_width
        upper = lower + group_width
        partial_value = jnp.zeros_like(total)
        for left, right in pairs:
            partial_value = partial_value + jnp.dot(left[:, lower:upper], right[:, lower:upper].T, preferred_element_type=jnp.float32)
        rounded = lax.optimization_barrier(partial_value.astype(jnp.bfloat16))
        total = total + rounded.astype(jnp.float32)
    return total

def norm_backward(states, gain_row, spread, grad_normed):
    widened = states.astype(jnp.float32)
    row_term = lax.optimization_barrier(jnp.sum(grad_normed * gain_row * widened, axis=-1, keepdims=True))
    result = gain_row * grad_normed / spread - widened * row_term / (D * spread ** 3)
    return result.astype(jnp.bfloat16)

def reference(segment_in, norm_gains, projections, live_counts, cotangent):
    normed_doc, spread_doc = normalize(segment_in[0], norm_gains[0])
    normed_sum, spread_sum = normalize(segment_in[1], norm_gains[1])
    w_key = projections[0, :, 0, :]
    w_value = projections[0, :, 1, :]
    w_query = projections[1, :, 0, :]
    w_out = projections[1, :, 1, :]
    keys = jnp.dot(normed_doc, w_key, preferred_element_type=jnp.float32).astype(jnp.bfloat16)
    values = jnp.dot(normed_doc, w_value, preferred_element_type=jnp.float32).astype(jnp.bfloat16)
    queries = jnp.dot(normed_sum, w_query, preferred_element_type=jnp.float32).astype(jnp.bfloat16)
    position = jnp.arange(B, dtype=jnp.int32)
    doc_live = position[None, :] < live_counts[0][:, None]
    sum_live = position[None, :] < live_counts[1][:, None]
    grad_out = jnp.dot(cotangent, w_out, preferred_element_type=jnp.float32).astype(jnp.bfloat16)
    grad_out = jnp.where(sum_live.reshape(-1)[:, None], grad_out, jnp.zeros_like(grad_out))
    key_blocks = keys.reshape(N_BLK, B, H, DH)
    value_blocks = values.reshape(N_BLK, B, H, DH)
    query_blocks = queries.reshape(N_BLK, B, H, DH)
    grad_blocks = grad_out.reshape(N_BLK, B, H, DH)

    def block_step(carry, block):
        key_acc, value_acc = carry
        raw_order = block - jnp.arange(WIN, dtype=jnp.int32)
        present = raw_order >= 0
        order = jnp.maximum(raw_order, 0).astype(jnp.int32)
        win_keys = key_blocks[order].reshape(WIN * B, H, DH).astype(jnp.float32)
        win_values = value_blocks[order].reshape(WIN * B, H, DH).astype(jnp.float32)
        live = (doc_live[order] & present[:, None]).reshape(-1)
        query_rows = query_blocks[block].astype(jnp.float32)
        scores = jnp.einsum('qhd,khd->hqk', query_rows, win_keys) * SCALE
        scores = jnp.where(live[None, None, :], scores, NEGATIVE)
        row_max = lax.optimization_barrier(jnp.max(scores, axis=-1, keepdims=True))
        expo = jnp.exp(scores - row_max)
        probs = expo / lax.optimization_barrier(jnp.sum(expo, axis=-1, keepdims=True))
        probs_low = probs.astype(jnp.bfloat16).astype(jnp.float32)
        attended = jnp.einsum('hqk,khd->qhd', probs_low, win_values).astype(jnp.bfloat16)
        query_live = sum_live[block]
        attended = jnp.where(query_live[:, None, None], attended, jnp.zeros_like(attended))
        grad_rows = grad_blocks[block].astype(jnp.float32)
        grad_probs = jnp.einsum('qhd,khd->hqk', grad_rows, win_values)
        row_delta = lax.optimization_barrier(jnp.sum(probs * grad_probs, axis=-1, keepdims=True))
        grad_scores = (probs * (grad_probs - row_delta)).astype(jnp.bfloat16).astype(jnp.float32)
        grad_queries = (SCALE * jnp.einsum('hqk,khd->qhd', grad_scores, win_keys)).astype(jnp.bfloat16)
        key_part = (SCALE * jnp.einsum('hqk,qhd->khd', grad_scores, query_rows)).reshape(WIN, B, H, DH)
        value_part = jnp.einsum('hqk,qhd->khd', probs_low, grad_rows).reshape(WIN, B, H, DH)
        key_acc = key_acc.at[order].add(key_part)
        value_acc = value_acc.at[order].add(value_part)
        return ((key_acc, value_acc), (attended, grad_queries))
    empty = jnp.zeros((N_BLK, B, H, DH), jnp.float32)
    (key_acc, value_acc), (attended, grad_queries) = lax.scan(block_step, (empty, empty), jnp.arange(N_BLK, dtype=jnp.int32))
    attended = attended.reshape(ROWS, H * DH)
    grad_queries = grad_queries.reshape(ROWS, H * DH)
    grad_keys = key_acc.reshape(ROWS, H * DH).astype(jnp.bfloat16)
    grad_values = value_acc.reshape(ROWS, H * DH).astype(jnp.bfloat16)
    layer_out = grouped_product([(attended, w_out)]).astype(jnp.bfloat16)
    grad_doc = grouped_product([(grad_keys, w_key), (grad_values, w_value)])
    grad_sum = grouped_product([(grad_queries, w_query)])
    segment_out = jnp.stack([normed_doc, layer_out])
    state_grads = jnp.stack([norm_backward(segment_in[0], norm_gains[0], spread_doc, grad_doc), norm_backward(segment_in[1], norm_gains[1], spread_sum, grad_sum)])
    return (segment_out, state_grads)
```

```python
import jax
import jax.numpy as jnp
from jax import lax
from jax.experimental import pallas as pl
from jax.experimental.pallas import tpu as pltpu
from jax.sharding import PartitionSpec as P

MESH = pl.DeviceIdType.MESH
F32 = jnp.float32
BF16 = jnp.bfloat16
EPSILON = 1e-06
SCALE = 0.125
NEGATIVE = -1e30
NT = (((1,), (1,)), ((), ()))
TN = (((0,), (0,)), ((), ()))
ROWS = 256
HALF = 128
WIDTH = 4096
SLICE = 1024
GROUP = 512
SLAB = ROWS + 16


def kernel(
    live_ref, x_hbm, gain_hbm, w_hbm, cot_hbm,
    seg_hbm, grad_hbm,
    states, gains, normed, rspread, wraw, wcat, acc, cot,
    kvsend, qsend, dsend, docs, qbuf, dbuf,
    sbuf, pbuf, dpbuf, gacc, osend, dqsend, obuf, dqbuf,
    zout, zin, gout, gbuf,
    left, lpart, lfar, lin, gpart, gfar, gin,
    rterm, rsend, rin, lout, gfin,
    load_sem, w_sem, loc_sem, out_sem,
    cot_s, cot_r, kv_s, doc_r, q_s, q_r, d_s, d_r, z_s, z_r,
    o_s, o_r, dq_s, dq_r, zg_s, zg_r, g_s, g_r,
    l_s, l_r, rs_s, rs_r, rt_s, rt_r,
):
    seg = lax.axis_index("segment")
    blk = lax.axis_index("blk")
    mp = lax.axis_index("mp")
    z = blk // 4
    quad = lax.rem(blk, 4)
    me = seg * 4 + quad
    n_z = lax.axis_size("blk") // 4
    z_up = lax.rem(z + 1, n_z)
    z_dn = lax.rem(z + n_z - 1, n_z)
    y_r, y_l, y_far = lax.rem(mp + 1, 4), lax.rem(mp + 3, 4), lax.rem(mp + 2, 4)

    def peer(t):
        return (t // 4, z * 4 + lax.rem(t, 4), mp)

    def at_y(y):
        return (seg, blk, y)

    def at_z(zz):
        return (seg, zz * 4 + quad, mp)

    def remote(src, dst, send, recv, to):
        return pltpu.make_async_remote_copy(
            src_ref=src, dst_ref=dst, send_sem=send, recv_sem=recv,
            device_id=to, device_id_type=MESH,
        )

    x_load = pltpu.make_async_copy(x_hbm.at[0], states, load_sem.at[0])
    g_load = pltpu.make_async_copy(gain_hbm, gains, load_sem.at[1])
    c_load = pltpu.make_async_copy(cot_hbm, cot.at[mp], load_sem.at[2])
    x_load.start()
    g_load.start()

    @pl.when(seg == 1)
    def _():
        c_load.start()

    def w_load(c):
        rows = pl.ds(pl.multiple_of(c * SLICE, SLICE), SLICE)
        return pltpu.make_async_copy(w_hbm.at[0, rows], wraw.at[rows], w_sem.at[c])

    for c in range(4):
        w_load(c).start()

    barrier = pltpu.get_barrier_semaphore()
    for k in range(1, 8):
        pl.semaphore_signal(barrier, inc=1, device_id=peer(lax.rem(me + k, 8)), device_id_type=MESH)
    for to in (at_y(y_r), at_y(y_l), at_y(y_far), at_z(z_up), at_z(z_dn)):
        pl.semaphore_signal(barrier, inc=1, device_id=to, device_id_type=MESH)
    pl.semaphore_wait(barrier, 12)

    top, bottom = pl.ds(0, HALF), pl.ds(HALF, HALF)

    def cot_copy(n):
        own_r = lambda h: (cot.at[mp, h], at_y(y_r))
        own_l = lambda h: (cot.at[mp, h], at_y(y_l))
        ref, to = [
            own_r(top), own_r(bottom), own_l(bottom), own_l(top),
            (cot.at[y_l, top], at_y(y_r)), (cot.at[y_r, bottom], at_y(y_l)),
        ][n]
        return remote(ref, ref, cot_s.at[n], cot_r.at[n], to)

    def cot_recv(n):
        ref = [
            cot.at[y_l, top], cot.at[y_l, bottom], cot.at[y_r, bottom], cot.at[y_r, top],
            cot.at[y_far, top], cot.at[y_far, bottom],
        ][n]
        remote(ref, ref, cot_s.at[n], cot_r.at[n], at_y(y_r)).wait_recv()

    @pl.when(seg == 1)
    def _():
        c_load.wait()
        for n in (0, 2, 1, 3):
            cot_copy(n).start()

    x_load.wait()
    g_load.wait()

    @pl.loop(0, 8)
    def _(i):
        rows = pl.ds(pl.multiple_of(i * 32, 32), 32)
        x = states[rows].astype(F32)
        inverse = 1.0 / jnp.sqrt(jnp.mean(x * x, axis=-1, keepdims=True) + EPSILON)
        rspread[rows] = jnp.broadcast_to(inverse, (32, 128))
        normed[rows] = (x * inverse * gains[...]).astype(BF16)

    own_columns = pl.ds(pl.multiple_of(mp * SLICE, SLICE), SLICE)
    normed_out = pltpu.make_async_copy(normed.at[:, own_columns], seg_hbm.at[0], out_sem.at[0])

    @pl.when(seg == 0)
    def _():
        normed_out.start()

    acc[...] = jnp.zeros_like(acc)

    @pl.loop(0, 4)
    def _(c):
        w_load(c).wait()

        @pl.loop(0, 4)
        def _(j):
            rows = pl.ds(pl.multiple_of(c * SLICE + j * 256, 256), 256)
            wcat[rows] = wraw[rows].reshape(256, 2 * GROUP)

        rows = pl.ds(pl.multiple_of(c * SLICE, SLICE), SLICE)

        @pl.when(seg == 0)
        def _():
            acc[...] += jnp.dot(normed[:, rows], wcat[rows], preferred_element_type=F32)

        @pl.when(seg == 1)
        def _():
            acc[:, :GROUP] += jnp.dot(
                normed[:, rows], wcat[rows, :GROUP], preferred_element_type=F32
            )

    def low_half(rows):
        return lax.broadcasted_iota(jnp.int32, (rows, 128), 1) < 64

    def exchange(a, b):
        low = low_half(a.shape[0])
        return jnp.where(low, a, pltpu.roll(b, 64, 1)), jnp.where(low, pltpu.roll(a, 64, 1), b)

    row_live = lax.broadcasted_iota(jnp.int32, (ROWS, 128), 0) < live_ref[1, 0]

    def kv_copy(t):
        return remote(kvsend.at[t], docs.at[3 + quad], kv_s.at[t], doc_r.at[3 + quad], peer(t))

    def q_copy(t):
        return remote(qsend.at[t], qbuf.at[quad], q_s.at[t], q_r.at[quad], peer(t))

    def d_copy(t):
        return remote(dsend.at[t], dbuf.at[quad], d_s.at[t], d_r.at[quad], peer(t))

    kv_own = pltpu.make_async_copy(kvsend.at[me], docs.at[3 + quad], loc_sem.at[0])
    q_own = pltpu.make_async_copy(qsend.at[me], qbuf.at[quad], loc_sem.at[0])
    d_own = pltpu.make_async_copy(dsend.at[me], dbuf.at[quad], loc_sem.at[1])

    @pl.when(seg == 0)
    def _():
        count = jnp.full((16, 128), live_ref[0, 0], jnp.int32).astype(F32).astype(BF16)
        for g in range(4):
            keys = acc[:, g * 128:(g + 1) * 128]
            values = acc[:, GROUP + g * 128:GROUP + (g + 1) * 128]
            even, odd = exchange(keys, values)
            kvsend[2 * g, :ROWS] = even.astype(BF16)
            kvsend[2 * g + 1, :ROWS] = odd.astype(BF16)
            kvsend[2 * g, ROWS:] = count
            kvsend[2 * g + 1, ROWS:] = count
        for k in range(1, 8):
            kv_copy(lax.rem(me + k, 8)).start()
        kv_own.start()

    @pl.when(seg == 1)
    def _():
        for g in range(4):
            pair = acc[:, g * 128:(g + 1) * 128]
            even, odd = exchange(pair[:HALF], pair[HALF:])
            qsend[2 * g] = even.astype(BF16)
            qsend[2 * g + 1] = odd.astype(BF16)
        for k in range(1, 8):
            q_copy(lax.rem(me + k, 8)).start()
        q_own.start()
        cot_recv(0)
        cot_copy(4).start()
        cot_recv(2)
        cot_copy(5).start()

    def z_copy(s):
        return remote(docs.at[s + 4], docs.at[s], z_s.at[s], z_r.at[s], at_z(z_up))

    def z_recv(s):
        remote(docs.at[s], docs.at[s], z_s.at[s], z_r.at[s], at_z(z_up)).wait_recv()

    for j in (1, 2, 3, 0):
        @pl.when(me == j)
        def _():
            kv_own.wait()

        @pl.when(me != j)
        def _():
            remote(docs.at[3 + j], docs.at[3 + j], kv_s.at[0], doc_r.at[3 + j], peer(j)).wait_recv()

        if j > 0:
            z_copy(j - 1).start()

    def from_summary(buf, recv, own, i):
        @pl.when(me == 4 + i)
        def _():
            own.wait()

        @pl.when(me != 4 + i)
        def _():
            remote(buf.at[i], buf.at[i], recv.at[i], recv.at[i], peer(4 + i)).wait_recv()

    def query(i):
        slab = qbuf[i].astype(F32)
        low = low_half(HALF)
        a = jnp.where(low, slab, 0.0)
        b = jnp.where(low, pltpu.roll(slab, 64, 1), 0.0)
        return jnp.concatenate([a, b], 0).astype(BF16)

    def gradient(i):
        slab = dbuf[i].astype(F32)
        low = low_half(HALF)
        a = jnp.where(low, 0.0, pltpu.roll(slab, 64, 1))
        b = jnp.where(low, 0.0, slab)
        return jnp.concatenate([a, b], 0).astype(BF16)

    def o_copy(i):
        return remote(osend.at[i], obuf.at[me], o_s.at[i], o_r.at[me], peer(4 + i))

    def dq_copy(i):
        return remote(dqsend.at[i], dqbuf.at[me], dq_s.at[i], dq_r.at[me], peer(4 + i))

    def o_own(i):
        return pltpu.make_async_copy(osend.at[i], obuf.at[me], loc_sem.at[2])

    def dq_own(i):
        return pltpu.make_async_copy(dqsend.at[i], dqbuf.at[me], loc_sem.at[3])

    @pl.loop(0, 4)
    def _(n):
        i = 3 - n

        @pl.when(i < 3)
        def _():
            z_recv(i)

        from_summary(qbuf, q_r, q_own, i)
        q0 = query(i)
        position = lax.broadcasted_iota(jnp.int32, (ROWS, ROWS), 0).astype(F32)
        peak = jnp.full((1, ROWS), NEGATIVE, F32)
        for j in range(4):
            s = lax.dot_general(docs[i + j, :ROWS], q0, NT, preferred_element_type=F32) * SCALE
            count = docs[i + j, ROWS:].astype(F32)[:1]
            count = jnp.where(4 * z - 3 + i + j >= 0, count, 0.0)
            count = jnp.concatenate([count, count], 1)
            s = jnp.where(position < count, s, NEGATIVE)
            sbuf[i, j] = s
            peak = jnp.maximum(peak, jnp.max(s, axis=0, keepdims=True))
        total = jnp.zeros((1, ROWS), F32)
        for j in range(4):
            e = jnp.exp(sbuf[i, j] - peak)
            sbuf[i, j] = e
            total = total + jnp.sum(e, axis=0, keepdims=True)
        share = 1.0 / total
        out = jnp.zeros((128, ROWS), F32)
        for j in range(4):
            probs = sbuf[i, j] * share
            sbuf[i, j] = probs
            low = probs.astype(BF16)
            pbuf[i, j] = low
            out = out + lax.dot_general(docs[i + j, :ROWS], low, TN, preferred_element_type=F32)
        out = out.T
        osend[i] = jnp.where(
            low_half(HALF), pltpu.roll(out[:HALF], 64, 1), out[HALF:]
        ).astype(BF16)

        @pl.when(me != 4 + i)
        def _():
            o_copy(i).start()

        @pl.when(me == 4 + i)
        def _():
            o_own(i).start()

    def collect(buf, recv, own, start, masked):
        for h in range(8):
            @pl.when(me == h)
            def _():
                own(quad).wait()

            @pl.when(me != h)
            def _():
                remote(buf.at[h], buf.at[h], recv.at[h], recv.at[h], peer(h)).wait_recv()
        for g in range(4):
            a, b = exchange(buf[2 * g].astype(F32), buf[2 * g + 1].astype(F32))
            pair = jnp.concatenate([a, b], 0)
            if masked:
                pair = jnp.where(row_live, pair, 0.0)
            left[:, start + g * 128:start + (g + 1) * 128] = pair.astype(BF16)

    def piece(columns, y, part, with_rows):
        @pl.loop(0, 4)
        def _(j):
            rows = pl.ds(pl.multiple_of(y * SLICE + j * 256, 256), 256)
            value = lax.dot_general(
                left[:, columns], wcat[rows, columns], NT, preferred_element_type=F32
            ).astype(BF16)
            part[y, :, pl.ds(pl.multiple_of(j * 256, 256), 256)] = value
            if with_rows:
                term = value.astype(F32) * (states[:, rows].astype(F32) * gains[:, rows])
                rterm[...] += term[:, :128] + term[:, 128:]

    def rs_copy(n, part, far, into, send, recv):
        src, dst, y = [
            (part.at[y_far, top], far.at[0], y_r),
            (part.at[y_far, bottom], far.at[1], y_l),
            (part.at[y_r, bottom], into.at[0, bottom], y_r),
            (part.at[y_r, top], into.at[0, top], y_r),
            (part.at[y_l, top], into.at[1, top], y_l),
            (part.at[y_l, bottom], into.at[1, bottom], y_l),
        ][n]
        return remote(src, dst, send.at[n], recv.at[n], at_y(y))

    def rs_recv(n, part, far, into, send, recv):
        dst = [
            far.at[0], far.at[1], into.at[0, bottom], into.at[0, top],
            into.at[1, top], into.at[1, bottom],
        ][n]
        remote(dst, dst, send.at[n], recv.at[n], at_y(y_r)).wait_recv()

    def rs_begin(columns, with_rows, args):
        part = args[0]
        piece(columns, y_far, part, with_rows)
        rs_copy(0, *args).start()
        rs_copy(1, *args).start()
        piece(columns, y_r, part, with_rows)
        rs_copy(2, *args).start()
        piece(columns, y_l, part, with_rows)
        rs_copy(4, *args).start()
        piece(columns, mp, part, with_rows)

    def rs_middle(args):
        part, far = args[:2]
        rs_recv(0, *args)
        part[y_r, top] = (part[y_r, top].astype(F32) + far[0].astype(F32)).astype(BF16)
        rs_copy(3, *args).start()
        rs_recv(1, *args)
        part[y_l, bottom] = (part[y_l, bottom].astype(F32) + far[1].astype(F32)).astype(BF16)
        rs_copy(5, *args).start()

    def rs_wait(args):
        for n in (2, 4, 3, 5):
            rs_recv(n, *args)

    l_args = (lpart, lfar, lin, l_s, l_r)
    g_args = (gpart, gfar, gin, rs_s, rs_r)
    first, second = pl.ds(0, GROUP), pl.ds(GROUP, GROUP)

    @pl.when(seg == 1)
    def _():
        for n in (1, 3, 4, 5):
            cot_recv(n)
        acc[:, GROUP:] = jnp.zeros((ROWS, GROUP), F32)

        @pl.loop(0, 4)
        def _(c):
            rows = pl.ds(pl.multiple_of(c * SLICE, SLICE), SLICE)
            acc[:, GROUP:] += jnp.dot(cot[c], wcat[rows, GROUP:], preferred_element_type=F32)

        for g in range(4):
            pair = jnp.where(row_live, acc[:, GROUP + g * 128:GROUP + (g + 1) * 128], 0.0)
            even, odd = exchange(pair[:HALF], pair[HALF:])
            dsend[2 * g] = even.astype(BF16)
            dsend[2 * g + 1] = odd.astype(BF16)
        for k in range(1, 8):
            d_copy(lax.rem(me + k, 8)).start()
        d_own.start()
        collect(obuf, o_r, o_own, GROUP, True)
        rs_begin(second, False, l_args)

    gacc[...] = jnp.zeros_like(gacc)

    def zg_copy(s):
        return remote(zout.at[s], zin.at[s], zg_s.at[s], zg_r.at[s], at_z(z_dn))

    @pl.loop(0, 4)
    def _(i):
        from_summary(dbuf, d_r, d_own, i)
        q0 = query(i)
        d0 = gradient(i)
        qd = q0 + d0
        delta = jnp.zeros((1, ROWS), F32)
        for j in range(4):
            dp = lax.dot_general(docs[i + j, :ROWS], d0, NT, preferred_element_type=F32)
            dpbuf[j] = dp
            delta = delta + jnp.sum(sbuf[i, j] * dp, axis=0, keepdims=True)
        out = jnp.zeros((128, ROWS), F32)
        low = low_half(ROWS)
        for j in range(4):
            ds = (sbuf[i, j] * (dpbuf[j] - delta)).astype(BF16)
            out = out + lax.dot_general(docs[i + j, :ROWS], ds, TN, preferred_element_type=F32)
            gk = jnp.dot(ds, qd, preferred_element_type=F32)
            gv = jnp.dot(pbuf[i, j], qd, preferred_element_type=F32)
            gacc[i + j] += jnp.where(low, SCALE * gk, gv)
        out = (SCALE * out).T
        dqsend[i] = jnp.where(
            low_half(HALF), out[:HALF], pltpu.roll(out[HALF:], 64, 1)
        ).astype(BF16)

        @pl.when(me != 4 + i)
        def _():
            dq_copy(i).start()

        @pl.when(me == 4 + i)
        def _():
            dq_own(i).start()

        @pl.when(i < 3)
        def _():
            zout[i] = gacc[i].astype(BF16)
            zg_copy(i).start()

    def g_copy(j):
        return remote(gout.at[j], gbuf.at[me], g_s.at[j], g_r.at[me], peer(j))

    def g_own(j):
        return pltpu.make_async_copy(gout.at[j], gbuf.at[me], loc_sem.at[2])

    for j in range(4):
        total = gacc[3 + j]
        if j > 0:
            remote(zin.at[j - 1], zin.at[j - 1], zg_s.at[0], zg_r.at[j - 1], at_z(z_up)).wait_recv()
            total = total + zin[j - 1].astype(F32)
        gout[j] = total.astype(BF16)

        @pl.when(me != j)
        def _():
            g_copy(j).start()

        @pl.when(me == j)
        def _():
            g_own(j).start()

    rterm[...] = jnp.zeros_like(rterm)

    @pl.when(seg == 1)
    def _():
        rs_middle(l_args)
        collect(dqbuf, dq_r, dq_own, 0, False)
        rs_begin(first, True, g_args)

    @pl.when(seg == 0)
    def _():
        for h in range(8):
            @pl.when(me == h)
            def _():
                g_own(quad).wait()

            @pl.when(me != h)
            def _():
                remote(gbuf.at[h], gbuf.at[h], g_r.at[h], g_r.at[h], peer(h)).wait_recv()
        for g in range(4):
            a, b = exchange(gbuf[2 * g].astype(F32), gbuf[2 * g + 1].astype(F32))
            left[:, g * 128:(g + 1) * 128] = a.astype(BF16)
            left[:, GROUP + g * 128:GROUP + (g + 1) * 128] = b.astype(BF16)
        rs_begin(pl.ds(0, 2 * GROUP), True, g_args)

    rsend[...] = jnp.broadcast_to(jnp.sum(rterm[...].T, axis=0, keepdims=True), (8, ROWS))

    def rt_copy(n, y):
        return remote(rsend, rin.at[n], rt_s.at[n], rt_r.at[n], at_y(y))

    for n, y in enumerate((y_r, y_l, y_far)):
        rt_copy(n, y).start()

    rs_middle(g_args)

    layer_out = pltpu.make_async_copy(lout, seg_hbm.at[0], out_sem.at[0])

    @pl.when(seg == 1)
    def _():
        rs_wait(l_args)

        @pl.loop(0, 8)
        def _(i):
            rows = pl.ds(pl.multiple_of(i * 32, 32), 32)
            value = lpart[mp, rows].astype(F32) + lin[0, rows].astype(F32) + lin[1, rows].astype(F32)
            lout[rows] = value.astype(BF16)

        layer_out.start()

    for n in range(3):
        remote(rin.at[n], rin.at[n], rt_s.at[n], rt_r.at[n], at_y(y_r)).wait_recv()
    sums = (rsend[...] + rin[0]) + (rin[1] + rin[2])
    rterm[...] = jnp.broadcast_to(sums[:1], (128, ROWS)).T

    rs_wait(g_args)

    @pl.loop(0, 8)
    def _(i):
        rows = pl.ds(pl.multiple_of(i * 32, 32), 32)
        value = gpart[mp, rows].astype(F32) + gin[0, rows].astype(F32) + gin[1, rows].astype(F32)
        inverse = rspread[rows]
        factor = rterm[rows] * (inverse * inverse * inverse) * (1.0 / WIDTH)
        gain = gains[:, own_columns]
        x = states[rows, own_columns].astype(F32)
        gfin[rows] = (gain * value * inverse[:, :1] - x * factor[:, :1]).astype(BF16)

    grad_out = pltpu.make_async_copy(gfin, grad_hbm.at[0], out_sem.at[1])
    grad_out.start()

    @pl.when(seg == 0)
    def _():
        normed_out.wait()
        for k in range(1, 8):
            kv_copy(lax.rem(me + k, 8)).wait_send()

    @pl.when(seg == 1)
    def _():
        layer_out.wait()
        for n in range(6):
            cot_copy(n).wait_send()
            rs_copy(n, *l_args).wait_send()
        for k in range(1, 8):
            q_copy(lax.rem(me + k, 8)).wait_send()
            d_copy(lax.rem(me + k, 8)).wait_send()

    for s in range(3):
        z_copy(s).wait_send()
        zg_copy(s).wait_send()
    for i in range(4):
        @pl.when(me != 4 + i)
        def _():
            o_copy(i).wait_send()
            dq_copy(i).wait_send()

        @pl.when(me != i)
        def _():
            g_copy(i).wait_send()
    for n in range(6):
        rs_copy(n, *g_args).wait_send()
    for n, y in enumerate((y_r, y_l, y_far)):
        rt_copy(n, y).wait_send()
    grad_out.wait()


def per_device(segment_in, norm_gains, projections, live_counts, cotangent):
    dma = lambda n: pltpu.SemaphoreType.DMA((n,))
    vmem = pltpu.VMEM
    shape = jax.ShapeDtypeStruct((1, ROWS, SLICE), BF16)
    hbm = pl.BlockSpec(memory_space=pl.ANY)
    return pl.pallas_call(
        kernel,
        name="window_attention",
        out_shape=(shape, shape),
        in_specs=[pl.BlockSpec(memory_space=pltpu.SMEM)] + [hbm] * 4,
        out_specs=(hbm, hbm),
        scratch_shapes=[
            vmem((ROWS, WIDTH), BF16),
            vmem((1, WIDTH), F32),
            vmem((ROWS, WIDTH), BF16),
            vmem((ROWS, 128), F32),
            vmem((WIDTH, 2, GROUP), BF16),
            vmem((WIDTH, 2 * GROUP), BF16),
            vmem((ROWS, 2 * GROUP), F32),
            vmem((4, ROWS, SLICE), BF16),
            vmem((8, SLAB, 128), BF16),
            vmem((8, HALF, 128), BF16),
            vmem((8, HALF, 128), BF16),
            vmem((7, SLAB, 128), BF16),
            vmem((4, HALF, 128), BF16),
            vmem((4, HALF, 128), BF16),
            vmem((4, 4, ROWS, ROWS), F32),
            vmem((4, 4, ROWS, ROWS), BF16),
            vmem((4, ROWS, ROWS), F32),
            vmem((7, ROWS, 128), F32),
            vmem((4, HALF, 128), BF16),
            vmem((4, HALF, 128), BF16),
            vmem((8, HALF, 128), BF16),
            vmem((8, HALF, 128), BF16),
            vmem((3, ROWS, 128), BF16),
            vmem((3, ROWS, 128), BF16),
            vmem((4, ROWS, 128), BF16),
            vmem((8, ROWS, 128), BF16),
            vmem((ROWS, 2 * GROUP), BF16),
            vmem((4, ROWS, SLICE), BF16),
            vmem((2, HALF, SLICE), BF16),
            vmem((2, ROWS, SLICE), BF16),
            vmem((4, ROWS, SLICE), BF16),
            vmem((2, HALF, SLICE), BF16),
            vmem((2, ROWS, SLICE), BF16),
            vmem((ROWS, 128), F32),
            vmem((8, ROWS), F32),
            vmem((3, 8, ROWS), F32),
            vmem((ROWS, SLICE), BF16),
            vmem((ROWS, SLICE), BF16),
            dma(3), dma(4), dma(4), dma(2),
            dma(6), dma(6), dma(8), dma(7), dma(8), dma(4), dma(8), dma(4), dma(3), dma(3),
            dma(4), dma(8), dma(4), dma(8), dma(3), dma(3), dma(4), dma(8),
            dma(6), dma(6), dma(6), dma(6), dma(3), dma(3),
        ],
        compiler_params=pltpu.CompilerParams(
            collective_id=0, has_side_effects=True, vmem_limit_bytes=56 * 1024 * 1024
        ),
        cost_estimate=pl.CostEstimate(flops=10**10, bytes_accessed=12 * 2**20, transcendentals=2**20),
    )(live_counts, segment_in, norm_gains, projections, cotangent)


def solution(mesh):
    in_specs = (
        P("segment", "blk", None),
        P("segment", None),
        P("segment", None, None, "mp"),
        P(None, "blk"),
        P("blk", "mp"),
    )
    out_specs = (P("segment", "blk", "mp"), P("segment", "blk", "mp"))
    return jax.shard_map(
        per_device, mesh=mesh, in_specs=in_specs, out_specs=out_specs, check_vma=False
    )
```

```python
import jax
import jax.numpy as jnp
from jax import lax
from jax.experimental import pallas as pl
from jax.experimental.pallas import tpu as pltpu
from jax.sharding import PartitionSpec as P

MESH = pl.DeviceIdType.MESH
F32 = jnp.float32
BF16 = jnp.bfloat16
EPSILON = 1e-06
SCALE = 0.125
NEGATIVE = -1e30
NT = (((1,), (1,)), ((), ()))
TN = (((0,), (0,)), ((), ()))
ROWS = 256
HALF = 128
WIDTH = 4096
SLICE = 1024
GROUP = 512
SLAB = ROWS + 16


def kernel(
    live_ref, x_hbm, gain_hbm, w_hbm, cot_hbm,
    seg_hbm, grad_hbm,
    states, gains, normed, rspread, wraw, wcat, acc, cot,
    kvsend, qsend, dsend, docs, qbuf, dbuf,
    sbuf, pbuf, dpbuf, gacc, osend, dqsend, obuf, dqbuf,
    zout, zin, gout, gbuf,
    left, lpart, lfar, lin, gpart, gfar, gin,
    rterm, rsend, rin, lout, gfin,
    load_sem, w_sem, loc_sem, out_sem,
    cot_s, cot_r, kv_s, doc_r, q_s, q_r, d_s, d_r, z_s, z_r,
    o_s, o_r, dq_s, dq_r, zg_s, zg_r, g_s, g_r,
    l_s, l_r, rs_s, rs_r, rt_s, rt_r,
):
    seg = lax.axis_index("segment")
    blk = lax.axis_index("blk")
    mp = lax.axis_index("mp")
    z = blk // 4
    quad = lax.rem(blk, 4)
    me = seg * 4 + quad
    n_z = lax.axis_size("blk") // 4
    z_up = lax.rem(z + 1, n_z)
    z_dn = lax.rem(z + n_z - 1, n_z)
    y_r, y_l, y_far = lax.rem(mp + 1, 4), lax.rem(mp + 3, 4), lax.rem(mp + 2, 4)

    def peer(t):
        return (t // 4, z * 4 + lax.rem(t, 4), mp)

    def at_y(y):
        return (seg, blk, y)

    def at_z(zz):
        return (seg, zz * 4 + quad, mp)

    def remote(src, dst, send, recv, to):
        return pltpu.make_async_remote_copy(
            src_ref=src, dst_ref=dst, send_sem=send, recv_sem=recv,
            device_id=to, device_id_type=MESH,
        )

    x_load = pltpu.make_async_copy(x_hbm.at[0], states, load_sem.at[0])
    g_load = pltpu.make_async_copy(gain_hbm, gains, load_sem.at[1])
    c_load = pltpu.make_async_copy(cot_hbm, cot.at[mp], load_sem.at[2])
    x_load.start()
    g_load.start()

    @pl.when(seg == 1)
    def _():
        c_load.start()

    def w_load(c):
        rows = pl.ds(pl.multiple_of(c * SLICE, SLICE), SLICE)
        return pltpu.make_async_copy(w_hbm.at[0, rows], wraw.at[rows], w_sem.at[c])

    for c in range(4):
        w_load(c).start()

    barrier = pltpu.get_barrier_semaphore()
    for k in range(1, 8):
        pl.semaphore_signal(barrier, inc=1, device_id=peer(lax.rem(me + k, 8)), device_id_type=MESH)
    for to in (at_y(y_r), at_y(y_l), at_y(y_far), at_z(z_up), at_z(z_dn)):
        pl.semaphore_signal(barrier, inc=1, device_id=to, device_id_type=MESH)

    top, bottom = pl.ds(0, HALF), pl.ds(HALF, HALF)

    def cot_copy(n):
        own_r = lambda h: (cot.at[mp, h], at_y(y_r))
        own_l = lambda h: (cot.at[mp, h], at_y(y_l))
        ref, to = [
            own_r(top), own_r(bottom), own_l(bottom), own_l(top),
            (cot.at[y_l, top], at_y(y_r)), (cot.at[y_r, bottom], at_y(y_l)),
        ][n]
        return remote(ref, ref, cot_s.at[n], cot_r.at[n], to)

    def cot_recv(n):
        ref = [
            cot.at[y_l, top], cot.at[y_l, bottom], cot.at[y_r, bottom], cot.at[y_r, top],
            cot.at[y_far, top], cot.at[y_far, bottom],
        ][n]
        remote(ref, ref, cot_s.at[n], cot_r.at[n], at_y(y_r)).wait_recv()

    def norm(i):
        rows = pl.ds(pl.multiple_of(i * 32, 32), 32)
        x = states[rows].astype(F32)
        inverse = 1.0 / jnp.sqrt(jnp.mean(x * x, axis=-1, keepdims=True) + EPSILON)
        rspread[rows] = jnp.broadcast_to(inverse, (32, 128))
        normed[rows] = (x * inverse * gains[...]).astype(BF16)

    x_load.wait()
    g_load.wait()
    pl.loop(0, 4)(norm)
    pl.semaphore_wait(barrier, 12)

    @pl.when(seg == 1)
    def _():
        c_load.wait()
        for n in (0, 2, 1, 3):
            cot_copy(n).start()

    pl.loop(4, 8)(norm)

    own_columns = pl.ds(pl.multiple_of(mp * SLICE, SLICE), SLICE)
    normed_out = pltpu.make_async_copy(normed.at[:, own_columns], seg_hbm.at[0], out_sem.at[0])

    @pl.when(seg == 0)
    def _():
        normed_out.start()

    def low_half(rows):
        return lax.broadcasted_iota(jnp.int32, (rows, 128), 1) < 64

    def exchange(a, b):
        low = low_half(a.shape[0])
        return jnp.where(low, a, pltpu.roll(b, 64, 1)), jnp.where(low, pltpu.roll(a, 64, 1), b)

    row_live = lax.broadcasted_iota(jnp.int32, (ROWS, 128), 0) < live_ref[0, 1]

    def kv_copy(t):
        return remote(kvsend.at[t], docs.at[3 + quad], kv_s.at[t], doc_r.at[3 + quad], peer(t))

    def q_copy(t):
        return remote(qsend.at[t], qbuf.at[quad], q_s.at[t], q_r.at[quad], peer(t))

    def d_copy(t):
        return remote(dsend.at[t], dbuf.at[quad], d_s.at[t], d_r.at[quad], peer(t))

    kv_own = pltpu.make_async_copy(kvsend.at[me], docs.at[3 + quad], loc_sem.at[0])
    q_own = pltpu.make_async_copy(qsend.at[me], qbuf.at[quad], loc_sem.at[0])
    d_own = pltpu.make_async_copy(dsend.at[me], dbuf.at[quad], loc_sem.at[1])

    @pl.when(seg == 0)
    def _():
        for c in range(4):
            w_load(c).wait()
        count = jnp.full((16, 128), live_ref[0, 0], jnp.int32).astype(F32).astype(BF16)
        chip = quad // 2
        for pair in (2 + chip, 3 - chip, 1 - chip, chip):
            source = pl.ds(pl.multiple_of(pair * 128, 128), 128)
            columns = pl.ds(pl.multiple_of(pair * 256, 256), 256)

            @pl.loop(0, 16)
            def _(j):
                rows = pl.ds(pl.multiple_of(j * 256, 256), 256)
                wcat[rows, columns] = wraw[rows, :, source].reshape(256, 256)

            both = jnp.dot(normed[...], wcat[:, columns], preferred_element_type=F32)
            even, odd = exchange(both[:, :128], both[:, 128:])
            for k, slab in enumerate((even, odd)):
                t = 2 * pair + k
                kvsend[t, :ROWS] = slab.astype(BF16)
                kvsend[t, ROWS:] = count

                @pl.when(t != me)
                def _():
                    kv_copy(t).start()

                @pl.when(t == me)
                def _():
                    kv_own.start()

    @pl.when(seg == 1)
    def _():
        acc[...] = jnp.zeros_like(acc)

        @pl.loop(0, 4)
        def _(c):
            w_load(c).wait()

            @pl.loop(0, 4)
            def _(j):
                rows = pl.ds(pl.multiple_of(c * SLICE + j * 256, 256), 256)
                wcat[rows] = wraw[rows].reshape(256, 2 * GROUP)

            rows = pl.ds(pl.multiple_of(c * SLICE, SLICE), SLICE)
            acc[:, :GROUP] += jnp.dot(
                normed[:, rows], wcat[rows, :GROUP], preferred_element_type=F32
            )

        for g in range(4):
            pair = acc[:, g * 128:(g + 1) * 128]
            even, odd = exchange(pair[:HALF], pair[HALF:])
            qsend[2 * g] = even.astype(BF16)
            qsend[2 * g + 1] = odd.astype(BF16)
        for k in range(1, 8):
            q_copy(lax.rem(me + k, 8)).start()
        q_own.start()
        cot_recv(0)
        cot_copy(4).start()
        cot_recv(2)
        cot_copy(5).start()

    def z_copy(s):
        return remote(docs.at[s + 4], docs.at[s], z_s.at[s], z_r.at[s], at_z(z_up))

    def z_recv(s):
        remote(docs.at[s], docs.at[s], z_s.at[s], z_r.at[s], at_z(z_up)).wait_recv()

    for j in (3, 2, 1, 0):
        @pl.when(me == j)
        def _():
            kv_own.wait()

        @pl.when(me != j)
        def _():
            remote(docs.at[3 + j], docs.at[3 + j], kv_s.at[0], doc_r.at[3 + j], peer(j)).wait_recv()

        if j > 0:
            z_copy(j - 1).start()

    def from_summary(buf, recv, own, i):
        @pl.when(me == 4 + i)
        def _():
            own.wait()

        @pl.when(me != 4 + i)
        def _():
            remote(buf.at[i], buf.at[i], recv.at[i], recv.at[i], peer(4 + i)).wait_recv()

    def query(i):
        slab = qbuf[i].astype(F32)
        low = low_half(HALF)
        a = jnp.where(low, slab, 0.0)
        b = jnp.where(low, pltpu.roll(slab, 64, 1), 0.0)
        return jnp.concatenate([a, b], 0).astype(BF16)

    def gradient(i):
        slab = dbuf[i].astype(F32)
        low = low_half(HALF)
        a = jnp.where(low, 0.0, pltpu.roll(slab, 64, 1))
        b = jnp.where(low, 0.0, slab)
        return jnp.concatenate([a, b], 0).astype(BF16)

    def o_copy(i):
        return remote(osend.at[i], obuf.at[me], o_s.at[i], o_r.at[me], peer(4 + i))

    def dq_copy(i):
        return remote(dqsend.at[i], dqbuf.at[me], dq_s.at[i], dq_r.at[me], peer(4 + i))

    def o_own(i):
        return pltpu.make_async_copy(osend.at[i], obuf.at[me], loc_sem.at[2])

    def dq_own(i):
        return pltpu.make_async_copy(dqsend.at[i], dqbuf.at[me], loc_sem.at[3])

    @pl.loop(0, 4)
    def _(n):
        i = 3 - n

        @pl.when(i < 3)
        def _():
            z_recv(i)

        from_summary(qbuf, q_r, q_own, i)
        q0 = query(i)
        position = lax.broadcasted_iota(jnp.int32, (ROWS, ROWS), 0).astype(F32)
        peak = jnp.full((1, ROWS), NEGATIVE, F32)
        for j in range(4):
            s = lax.dot_general(docs[i + j, :ROWS], q0, NT, preferred_element_type=F32) * SCALE
            count = docs[i + j, ROWS:].astype(F32)[:1]
            count = jnp.where(4 * z - 3 + i + j >= 0, count, 0.0)
            count = jnp.concatenate([count, count], 1)
            s = jnp.where(position < count, s, NEGATIVE)
            sbuf[i, j] = s
            peak = jnp.maximum(peak, jnp.max(s, axis=0, keepdims=True))
        total = jnp.zeros((1, ROWS), F32)
        for j in range(4):
            e = jnp.exp(sbuf[i, j] - peak)
            sbuf[i, j] = e
            total = total + jnp.sum(e, axis=0, keepdims=True)
        share = 1.0 / total
        out = jnp.zeros((128, ROWS), F32)
        for j in range(4):
            probs = sbuf[i, j] * share
            sbuf[i, j] = probs
            low = probs.astype(BF16)
            pbuf[i, j] = low
            out = out + lax.dot_general(docs[i + j, :ROWS], low, TN, preferred_element_type=F32)
        out = out.T
        osend[i] = jnp.where(
            low_half(HALF), pltpu.roll(out[:HALF], 64, 1), out[HALF:]
        ).astype(BF16)

        @pl.when(me != 4 + i)
        def _():
            o_copy(i).start()

        @pl.when(me == 4 + i)
        def _():
            o_own(i).start()

    def collect(buf, recv, own, start, masked):
        for h in range(8):
            @pl.when(me == h)
            def _():
                own(quad).wait()

            @pl.when(me != h)
            def _():
                remote(buf.at[h], buf.at[h], recv.at[h], recv.at[h], peer(h)).wait_recv()
        for g in range(4):
            a, b = exchange(buf[2 * g].astype(F32), buf[2 * g + 1].astype(F32))
            pair = jnp.concatenate([a, b], 0)
            if masked:
                pair = jnp.where(row_live, pair, 0.0)
            left[:, start + g * 128:start + (g + 1) * 128] = pair.astype(BF16)

    def piece(columns, y, part, with_rows):
        @pl.loop(0, 4)
        def _(j):
            rows = pl.ds(pl.multiple_of(y * SLICE + j * 256, 256), 256)
            value = lax.dot_general(
                left[:, columns], wcat[rows, columns], NT, preferred_element_type=F32
            ).astype(BF16)
            part[y, :, pl.ds(pl.multiple_of(j * 256, 256), 256)] = value
            if with_rows:
                term = value.astype(F32) * (states[:, rows].astype(F32) * gains[:, rows])
                rterm[...] += term[:, :128] + term[:, 128:]

    def rs_copy(n, part, far, into, send, recv):
        src, dst, y = [
            (part.at[y_far, top], far.at[0], y_r),
            (part.at[y_far, bottom], far.at[1], y_l),
            (part.at[y_r, bottom], into.at[0, bottom], y_r),
            (part.at[y_r, top], into.at[0, top], y_r),
            (part.at[y_l, top], into.at[1, top], y_l),
            (part.at[y_l, bottom], into.at[1, bottom], y_l),
        ][n]
        return remote(src, dst, send.at[n], recv.at[n], at_y(y))

    def rs_recv(n, part, far, into, send, recv):
        dst = [
            far.at[0], far.at[1], into.at[0, bottom], into.at[0, top],
            into.at[1, top], into.at[1, bottom],
        ][n]
        remote(dst, dst, send.at[n], recv.at[n], at_y(y_r)).wait_recv()

    def rs_begin(columns, with_rows, args):
        part = args[0]
        piece(columns, y_far, part, with_rows)
        rs_copy(0, *args).start()
        rs_copy(1, *args).start()
        piece(columns, y_r, part, with_rows)
        rs_copy(2, *args).start()
        piece(columns, y_l, part, with_rows)
        rs_copy(4, *args).start()
        piece(columns, mp, part, with_rows)

    def rs_middle(args):
        part, far = args[:2]
        rs_recv(0, *args)
        part[y_r, top] = (part[y_r, top].astype(F32) + far[0].astype(F32)).astype(BF16)
        rs_copy(3, *args).start()
        rs_recv(1, *args)
        part[y_l, bottom] = (part[y_l, bottom].astype(F32) + far[1].astype(F32)).astype(BF16)
        rs_copy(5, *args).start()

    def rs_wait(args):
        for n in (2, 4, 3, 5):
            rs_recv(n, *args)

    l_args = (lpart, lfar, lin, l_s, l_r)
    g_args = (gpart, gfar, gin, rs_s, rs_r)
    first, second = pl.ds(0, GROUP), pl.ds(GROUP, GROUP)

    @pl.when(seg == 1)
    def _():
        for n in (1, 3):
            cot_recv(n)

        def gather_product(k):
            c = lax.rem(y_far + k, 4)
            rows = pl.ds(pl.multiple_of(c * SLICE, SLICE), SLICE)
            acc[:, GROUP:] += jnp.dot(cot[c], wcat[rows, GROUP:], preferred_element_type=F32)

        pl.loop(1, 4)(gather_product)
        for n in (4, 5):
            cot_recv(n)
        gather_product(0)

        for g in range(4):
            pair = jnp.where(row_live, acc[:, GROUP + g * 128:GROUP + (g + 1) * 128], 0.0)
            even, odd = exchange(pair[:HALF], pair[HALF:])
            dsend[2 * g] = even.astype(BF16)
            dsend[2 * g + 1] = odd.astype(BF16)
        for k in range(1, 8):
            d_copy(lax.rem(me + k, 8)).start()
        d_own.start()
        collect(obuf, o_r, o_own, GROUP, True)
        rs_begin(second, False, l_args)

    gacc[...] = jnp.zeros_like(gacc)

    def zg_copy(s):
        return remote(zout.at[s], zin.at[s], zg_s.at[s], zg_r.at[s], at_z(z_dn))

    @pl.loop(0, 4)
    def _(i):
        from_summary(dbuf, d_r, d_own, i)
        q0 = query(i)
        d0 = gradient(i)
        qd = q0 + d0
        delta = jnp.zeros((1, ROWS), F32)
        for j in range(4):
            dp = lax.dot_general(docs[i + j, :ROWS], d0, NT, preferred_element_type=F32)
            dpbuf[j] = dp
            delta = delta + jnp.sum(sbuf[i, j] * dp, axis=0, keepdims=True)
        out = jnp.zeros((128, ROWS), F32)
        low = low_half(ROWS)
        for j in range(4):
            ds = (sbuf[i, j] * (dpbuf[j] - delta)).astype(BF16)
            out = out + lax.dot_general(docs[i + j, :ROWS], ds, TN, preferred_element_type=F32)
            gk = jnp.dot(ds, qd, preferred_element_type=F32)
            gv = jnp.dot(pbuf[i, j], qd, preferred_element_type=F32)
            gacc[i + j] += jnp.where(low, SCALE * gk, gv)
        out = (SCALE * out).T
        dqsend[i] = jnp.where(
            low_half(HALF), out[:HALF], pltpu.roll(out[HALF:], 64, 1)
        ).astype(BF16)

        @pl.when(me != 4 + i)
        def _():
            dq_copy(i).start()

        @pl.when(me == 4 + i)
        def _():
            dq_own(i).start()

        @pl.when(i < 3)
        def _():
            zout[i] = gacc[i].astype(BF16)
            zg_copy(i).start()

    def g_copy(j):
        return remote(gout.at[j], gbuf.at[me], g_s.at[j], g_r.at[me], peer(j))

    def g_own(j):
        return pltpu.make_async_copy(gout.at[j], gbuf.at[me], loc_sem.at[2])

    for j in range(4):
        total = gacc[3 + j]
        if j > 0:
            remote(zin.at[j - 1], zin.at[j - 1], zg_s.at[0], zg_r.at[j - 1], at_z(z_up)).wait_recv()
            total = total + zin[j - 1].astype(F32)
        gout[j] = total.astype(BF16)

        @pl.when(me != j)
        def _():
            g_copy(j).start()

        @pl.when(me == j)
        def _():
            g_own(j).start()

    rterm[...] = jnp.zeros_like(rterm)

    @pl.when(seg == 1)
    def _():
        rs_middle(l_args)
        collect(dqbuf, dq_r, dq_own, 0, False)
        rs_begin(first, True, g_args)

    @pl.when(seg == 0)
    def _():
        for h in range(8):
            @pl.when(me == h)
            def _():
                g_own(quad).wait()

            @pl.when(me != h)
            def _():
                remote(gbuf.at[h], gbuf.at[h], g_r.at[h], g_r.at[h], peer(h)).wait_recv()
        for g in range(4):
            a, b = exchange(gbuf[2 * g].astype(F32), gbuf[2 * g + 1].astype(F32))
            left[:, g * 256:g * 256 + 128] = a.astype(BF16)
            left[:, g * 256 + 128:(g + 1) * 256] = b.astype(BF16)
        rs_begin(pl.ds(0, 2 * GROUP), True, g_args)

    rsend[...] = jnp.broadcast_to(jnp.sum(rterm[...].T, axis=0, keepdims=True), (8, ROWS))

    def rt_copy(n, y):
        return remote(rsend, rin.at[n], rt_s.at[n], rt_r.at[n], at_y(y))

    for n, y in enumerate((y_r, y_l, y_far)):
        rt_copy(n, y).start()

    rs_middle(g_args)

    layer_out = pltpu.make_async_copy(lout, seg_hbm.at[0], out_sem.at[0])

    @pl.when(seg == 1)
    def _():
        rs_wait(l_args)

        @pl.loop(0, 8)
        def _(i):
            rows = pl.ds(pl.multiple_of(i * 32, 32), 32)
            value = lpart[mp, rows].astype(F32) + lin[0, rows].astype(F32) + lin[1, rows].astype(F32)
            lout[rows] = value.astype(BF16)

        layer_out.start()

    for n in range(3):
        remote(rin.at[n], rin.at[n], rt_s.at[n], rt_r.at[n], at_y(y_r)).wait_recv()
    sums = (rsend[...] + rin[0]) + (rin[1] + rin[2])
    rterm[...] = jnp.broadcast_to(sums[:1], (128, ROWS)).T

    rs_wait(g_args)

    @pl.loop(0, 8)
    def _(i):
        rows = pl.ds(pl.multiple_of(i * 32, 32), 32)
        value = gpart[mp, rows].astype(F32) + gin[0, rows].astype(F32) + gin[1, rows].astype(F32)
        inverse = rspread[rows]
        factor = rterm[rows] * (inverse * inverse * inverse) * (1.0 / WIDTH)
        gain = gains[:, own_columns]
        x = states[rows, own_columns].astype(F32)
        gfin[rows] = (gain * value * inverse[:, :1] - x * factor[:, :1]).astype(BF16)

    grad_out = pltpu.make_async_copy(gfin, grad_hbm.at[0], out_sem.at[1])
    grad_out.start()

    @pl.when(seg == 0)
    def _():
        normed_out.wait()
        for k in range(1, 8):
            kv_copy(lax.rem(me + k, 8)).wait_send()

    @pl.when(seg == 1)
    def _():
        layer_out.wait()
        for n in range(6):
            cot_copy(n).wait_send()
            rs_copy(n, *l_args).wait_send()
        for k in range(1, 8):
            q_copy(lax.rem(me + k, 8)).wait_send()
            d_copy(lax.rem(me + k, 8)).wait_send()

    for s in range(3):
        z_copy(s).wait_send()
        zg_copy(s).wait_send()
    for i in range(4):
        @pl.when(me != 4 + i)
        def _():
            o_copy(i).wait_send()
            dq_copy(i).wait_send()

        @pl.when(me != i)
        def _():
            g_copy(i).wait_send()
    for n in range(6):
        rs_copy(n, *g_args).wait_send()
    for n, y in enumerate((y_r, y_l, y_far)):
        rt_copy(n, y).wait_send()
    grad_out.wait()


def deliver(seg_in, grad_in, seg_out, grad_out, sem):
    copies = [
        pltpu.make_async_copy(seg_in, seg_out, sem.at[0]),
        pltpu.make_async_copy(grad_in, grad_out, sem.at[1]),
    ]
    for copy in copies:
        copy.start()
    for copy in copies:
        copy.wait()


def per_device(segment_in, norm_gains, projections, live_counts, cotangent):
    dma = lambda n: pltpu.SemaphoreType.DMA((n,))
    vmem = pltpu.VMEM
    shape = jax.ShapeDtypeStruct((1, ROWS, SLICE), BF16)
    hbm = pl.BlockSpec(memory_space=pl.ANY)
    results = pl.pallas_call(
        kernel,
        name="window_attention",
        out_shape=(shape, shape),
        in_specs=[pl.BlockSpec(memory_space=pltpu.SMEM)] + [hbm] * 4,
        out_specs=(hbm, hbm),
        scratch_shapes=[
            vmem((ROWS, WIDTH), BF16),
            vmem((1, WIDTH), F32),
            vmem((ROWS, WIDTH), BF16),
            vmem((ROWS, 128), F32),
            vmem((WIDTH, 2, GROUP), BF16),
            vmem((WIDTH, 2 * GROUP), BF16),
            vmem((ROWS, 2 * GROUP), F32),
            vmem((4, ROWS, SLICE), BF16),
            vmem((8, SLAB, 128), BF16),
            vmem((8, HALF, 128), BF16),
            vmem((8, HALF, 128), BF16),
            vmem((7, SLAB, 128), BF16),
            vmem((4, HALF, 128), BF16),
            vmem((4, HALF, 128), BF16),
            vmem((4, 4, ROWS, ROWS), F32),
            vmem((4, 4, ROWS, ROWS), BF16),
            vmem((4, ROWS, ROWS), F32),
            vmem((7, ROWS, 128), F32),
            vmem((4, HALF, 128), BF16),
            vmem((4, HALF, 128), BF16),
            vmem((8, HALF, 128), BF16),
            vmem((8, HALF, 128), BF16),
            vmem((3, ROWS, 128), BF16),
            vmem((3, ROWS, 128), BF16),
            vmem((4, ROWS, 128), BF16),
            vmem((8, ROWS, 128), BF16),
            vmem((ROWS, 2 * GROUP), BF16),
            vmem((4, ROWS, SLICE), BF16),
            vmem((2, HALF, SLICE), BF16),
            vmem((2, ROWS, SLICE), BF16),
            vmem((4, ROWS, SLICE), BF16),
            vmem((2, HALF, SLICE), BF16),
            vmem((2, ROWS, SLICE), BF16),
            vmem((ROWS, 128), F32),
            vmem((8, ROWS), F32),
            vmem((3, 8, ROWS), F32),
            vmem((ROWS, SLICE), BF16),
            vmem((ROWS, SLICE), BF16),
            dma(3), dma(4), dma(4), dma(2),
            dma(6), dma(6), dma(8), dma(7), dma(8), dma(4), dma(8), dma(4), dma(3), dma(3),
            dma(4), dma(8), dma(4), dma(8), dma(3), dma(3), dma(4), dma(8),
            dma(6), dma(6), dma(6), dma(6), dma(3), dma(3),
        ],
        compiler_params=pltpu.CompilerParams(
            collective_id=0, has_side_effects=True, vmem_limit_bytes=56 * 1024 * 1024
        ),
        cost_estimate=pl.CostEstimate(flops=10**10, bytes_accessed=12 * 2**20, transcendentals=2**20),
    )(live_counts.reshape(1, 2), segment_in, norm_gains, projections, cotangent)
    return pl.pallas_call(
        deliver,
        name="deliver",
        out_shape=(shape, shape),
        in_specs=[hbm] * 2,
        out_specs=(hbm, hbm),
        scratch_shapes=[dma(2)],
    )(*results)


def solution(mesh):
    in_specs = (
        P("segment", "blk", None),
        P("segment", None),
        P("segment", None, None, "mp"),
        P(None, "blk"),
        P("blk", "mp"),
    )
    out_specs = (P("segment", "blk", "mp"), P("segment", "blk", "mp"))
    return jax.shard_map(
        per_device, mesh=mesh, in_specs=in_specs, out_specs=out_specs, check_vma=False
    )
```

```python
import jax
import jax.numpy as jnp
from jax import lax
from jax.experimental import pallas as pl
from jax.experimental.pallas import tpu as pltpu
from jax.sharding import PartitionSpec as P

MESH = pl.DeviceIdType.MESH
F32 = jnp.float32
BF16 = jnp.bfloat16
EPSILON = 1e-06
SCALE = 0.125
NEGATIVE = -1e30
NT = (((1,), (1,)), ((), ()))
TN = (((0,), (0,)), ((), ()))
ROWS = 256
HALF = 128
WIDTH = 4096
SLICE = 1024
GROUP = 512
SLAB = ROWS + 16


def kernel(
    live_ref, x_hbm, gain_hbm, w_hbm, cot_hbm,
    seg_hbm, grad_hbm,
    states, gains, normed, rspread, wraw, wcat, acc, cot,
    kvsend, qsend, dsend, docs, qbuf, dbuf,
    sbuf, pbuf, dpbuf, gacc, osend, dqsend, obuf, dqbuf,
    zout, zin, gout, gbuf,
    left, lpart, lfar, lin, gpart, gfar, gin,
    rterm, rsend, rin, lout, gfin,
    load_sem, w_sem, loc_sem, out_sem,
    cot_s, cot_r, kv_s, doc_r, q_s, q_r, d_s, d_r, z_s, z_r,
    o_s, o_r, dq_s, dq_r, zg_s, zg_r, g_s, g_r,
    l_s, l_r, rs_s, rs_r, rt_s, rt_r,
):
    seg = lax.axis_index("segment")
    blk = lax.axis_index("blk")
    mp = lax.axis_index("mp")
    z = blk // 4
    quad = lax.rem(blk, 4)
    me = seg * 4 + quad
    n_z = lax.axis_size("blk") // 4
    z_up = lax.rem(z + 1, n_z)
    z_dn = lax.rem(z + n_z - 1, n_z)
    y_r, y_l, y_far = lax.rem(mp + 1, 4), lax.rem(mp + 3, 4), lax.rem(mp + 2, 4)

    def peer(t):
        return (t // 4, z * 4 + lax.rem(t, 4), mp)

    def at_y(y):
        return (seg, blk, y)

    def at_z(zz):
        return (seg, zz * 4 + quad, mp)

    def remote(src, dst, send, recv, to):
        return pltpu.make_async_remote_copy(
            src_ref=src, dst_ref=dst, send_sem=send, recv_sem=recv,
            device_id=to, device_id_type=MESH,
        )

    x_load = pltpu.make_async_copy(x_hbm.at[0], states, load_sem.at[0])
    g_load = pltpu.make_async_copy(gain_hbm, gains, load_sem.at[1])
    c_load = pltpu.make_async_copy(cot_hbm, cot.at[mp], load_sem.at[2])
    x_load.start()
    g_load.start()

    @pl.when(seg == 1)
    def _():
        c_load.start()

    def w_load(c):
        rows = pl.ds(pl.multiple_of(c * SLICE, SLICE), SLICE)
        return pltpu.make_async_copy(w_hbm.at[0, rows], wraw.at[rows], w_sem.at[c])

    for c in range(4):
        w_load(c).start()

    barrier = pltpu.get_barrier_semaphore()
    for k in range(1, 8):
        pl.semaphore_signal(barrier, inc=1, device_id=peer(lax.rem(me + k, 8)), device_id_type=MESH)
    for to in (at_y(y_r), at_y(y_l), at_y(y_far), at_z(z_up), at_z(z_dn)):
        pl.semaphore_signal(barrier, inc=1, device_id=to, device_id_type=MESH)

    top, bottom = pl.ds(0, HALF), pl.ds(HALF, HALF)

    def cot_copy(n):
        own_r = lambda h: (cot.at[mp, h], at_y(y_r))
        own_l = lambda h: (cot.at[mp, h], at_y(y_l))
        ref, to = [
            own_r(top), own_r(bottom), own_l(bottom), own_l(top),
            (cot.at[y_l, top], at_y(y_r)), (cot.at[y_r, bottom], at_y(y_l)),
        ][n]
        return remote(ref, ref, cot_s.at[n], cot_r.at[n], to)

    def cot_recv(n):
        ref = [
            cot.at[y_l, top], cot.at[y_l, bottom], cot.at[y_r, bottom], cot.at[y_r, top],
            cot.at[y_far, top], cot.at[y_far, bottom],
        ][n]
        remote(ref, ref, cot_s.at[n], cot_r.at[n], at_y(y_r)).wait_recv()

    def norm(i):
        rows = pl.ds(pl.multiple_of(i * 32, 32), 32)
        x = states[rows].astype(F32)
        inverse = 1.0 / jnp.sqrt(jnp.mean(x * x, axis=-1, keepdims=True) + EPSILON)
        rspread[rows] = jnp.broadcast_to(inverse, (32, 128))
        normed[rows] = (x * inverse * gains[...]).astype(BF16)

    x_load.wait()
    g_load.wait()
    pl.loop(0, 4)(norm)

    @pl.when(seg == 1)
    def _():
        pl.semaphore_wait(barrier, 12)
        c_load.wait()
        for n in (0, 2):
            cot_copy(n).start()

    pl.loop(4, 8)(norm)

    own_columns = pl.ds(pl.multiple_of(mp * SLICE, SLICE), SLICE)
    normed_out = pltpu.make_async_copy(normed.at[:, own_columns], seg_hbm.at[0], out_sem.at[0])

    @pl.when(seg == 0)
    def _():
        normed_out.start()

    def low_half(rows):
        return lax.broadcasted_iota(jnp.int32, (rows, 128), 1) < 64

    def exchange(a, b):
        low = low_half(a.shape[0])
        return jnp.where(low, a, pltpu.roll(b, 64, 1)), jnp.where(low, pltpu.roll(a, 64, 1), b)

    row_live = lax.broadcasted_iota(jnp.int32, (ROWS, 128), 0) < live_ref[0, 1]

    def kv_copy(t):
        return remote(kvsend.at[t], docs.at[3 + quad], kv_s.at[t], doc_r.at[3 + quad], peer(t))

    def q_copy(t):
        return remote(qsend.at[t], qbuf.at[quad], q_s.at[t], q_r.at[quad], peer(t))

    def d_copy(t):
        return remote(dsend.at[t], dbuf.at[quad], d_s.at[t], d_r.at[quad], peer(t))

    kv_own = pltpu.make_async_copy(kvsend.at[me], docs.at[3 + quad], loc_sem.at[0])
    q_own = pltpu.make_async_copy(qsend.at[me], qbuf.at[quad], loc_sem.at[0])
    d_own = pltpu.make_async_copy(dsend.at[me], dbuf.at[quad], loc_sem.at[1])

    def spread_weights(c):
        w_load(c).wait()

        @pl.loop(0, 4)
        def _(j):
            rows = pl.ds(pl.multiple_of(c * SLICE + j * 256, 256), 256)
            wcat[rows] = wraw[rows].reshape(256, 2 * GROUP)

    @pl.when(seg == 0)
    def _():
        pl.loop(0, 4)(spread_weights)
        pl.semaphore_wait(barrier, 12)
        count = jnp.full((16, 128), live_ref[0, 0], jnp.int32).astype(F32).astype(BF16)
        for stage in (1, 0):
            start = stage * 256
            keys = jnp.dot(normed[...], wcat[:, start:start + 256], preferred_element_type=F32)
            start = GROUP + start
            values = jnp.dot(normed[...], wcat[:, start:start + 256], preferred_element_type=F32)
            for g in range(2):
                part = slice(g * 128, (g + 1) * 128)
                for k, slab in enumerate(exchange(keys[:, part], values[:, part])):
                    t = 4 * stage + 2 * g + k
                    kvsend[t, :ROWS] = slab.astype(BF16)
                    kvsend[t, ROWS:] = count
            for k in range(4):
                t = 4 * stage + lax.rem(quad + k, 4)
                if stage == 0 and k == 0:
                    kv_own.start()
                else:
                    kv_copy(t).start()

    @pl.when(seg == 1)
    def _():
        acc[...] = jnp.zeros_like(acc)

        @pl.loop(0, 4)
        def _(c):
            spread_weights(c)
            rows = pl.ds(pl.multiple_of(c * SLICE, SLICE), SLICE)
            acc[:, :GROUP] += jnp.dot(
                normed[:, rows], wcat[rows, :GROUP], preferred_element_type=F32
            )

        for g in range(4):
            pair = acc[:, g * 128:(g + 1) * 128]
            even, odd = exchange(pair[:HALF], pair[HALF:])
            qsend[2 * g] = even.astype(BF16)
            qsend[2 * g + 1] = odd.astype(BF16)
        for k in range(1, 8):
            q_copy(lax.rem(me + k, 8)).start()
        q_own.start()
        cot_recv(0)
        cot_recv(2)
        for n in (1, 3, 4, 5):
            cot_copy(n).start()

    def z_copy(s):
        return remote(docs.at[s + 4], docs.at[s], z_s.at[s], z_r.at[s], at_z(z_up))

    def z_recv(s):
        remote(docs.at[s], docs.at[s], z_s.at[s], z_r.at[s], at_z(z_up)).wait_recv()

    for j in (3, 2, 1, 0):
        @pl.when(me == j)
        def _():
            kv_own.wait()

        @pl.when(me != j)
        def _():
            remote(docs.at[3 + j], docs.at[3 + j], kv_s.at[0], doc_r.at[3 + j], peer(j)).wait_recv()

        if j > 0:
            z_copy(j - 1).start()

    def from_summary(buf, recv, own, i):
        @pl.when(me == 4 + i)
        def _():
            own.wait()

        @pl.when(me != 4 + i)
        def _():
            remote(buf.at[i], buf.at[i], recv.at[i], recv.at[i], peer(4 + i)).wait_recv()

    def query(i):
        slab = qbuf[i].astype(F32)
        low = low_half(HALF)
        a = jnp.where(low, slab, 0.0)
        b = jnp.where(low, pltpu.roll(slab, 64, 1), 0.0)
        return jnp.concatenate([a, b], 0).astype(BF16)

    def gradient(i):
        slab = dbuf[i].astype(F32)
        low = low_half(HALF)
        a = jnp.where(low, 0.0, pltpu.roll(slab, 64, 1))
        b = jnp.where(low, 0.0, slab)
        return jnp.concatenate([a, b], 0).astype(BF16)

    def o_copy(i):
        return remote(osend.at[i], obuf.at[me], o_s.at[i], o_r.at[me], peer(4 + i))

    def dq_copy(i):
        return remote(dqsend.at[i], dqbuf.at[me], dq_s.at[i], dq_r.at[me], peer(4 + i))

    def o_own(i):
        return pltpu.make_async_copy(osend.at[i], obuf.at[me], loc_sem.at[2])

    def dq_own(i):
        return pltpu.make_async_copy(dqsend.at[i], dqbuf.at[me], loc_sem.at[3])

    @pl.loop(0, 4)
    def _(n):
        i = 3 - n

        @pl.when(i < 3)
        def _():
            z_recv(i)

        from_summary(qbuf, q_r, q_own, i)
        q0 = query(i)
        position = lax.broadcasted_iota(jnp.int32, (ROWS, ROWS), 0).astype(F32)
        peak = jnp.full((1, ROWS), NEGATIVE, F32)
        for j in range(4):
            s = lax.dot_general(docs[i + j, :ROWS], q0, NT, preferred_element_type=F32) * SCALE
            count = docs[i + j, ROWS:].astype(F32)[:1]
            count = jnp.where(4 * z - 3 + i + j >= 0, count, 0.0)
            count = jnp.concatenate([count, count], 1)
            s = jnp.where(position < count, s, NEGATIVE)
            sbuf[i, j] = s
            peak = jnp.maximum(peak, jnp.max(s, axis=0, keepdims=True))
        total = jnp.zeros((1, ROWS), F32)
        for j in range(4):
            e = jnp.exp(sbuf[i, j] - peak)
            sbuf[i, j] = e
            total = total + jnp.sum(e, axis=0, keepdims=True)
        share = 1.0 / total
        out = jnp.zeros((128, ROWS), F32)
        for j in range(4):
            probs = sbuf[i, j] * share
            sbuf[i, j] = probs
            low = probs.astype(BF16)
            pbuf[i, j] = low
            out = out + lax.dot_general(docs[i + j, :ROWS], low, TN, preferred_element_type=F32)
        out = out.T
        osend[i] = jnp.where(
            low_half(HALF), pltpu.roll(out[:HALF], 64, 1), out[HALF:]
        ).astype(BF16)

        @pl.when(me != 4 + i)
        def _():
            o_copy(i).start()

        @pl.when(me == 4 + i)
        def _():
            o_own(i).start()

    def collect(buf, recv, own, start, masked):
        for h in range(8):
            @pl.when(me == h)
            def _():
                own(quad).wait()

            @pl.when(me != h)
            def _():
                remote(buf.at[h], buf.at[h], recv.at[h], recv.at[h], peer(h)).wait_recv()
        for g in range(4):
            a, b = exchange(buf[2 * g].astype(F32), buf[2 * g + 1].astype(F32))
            pair = jnp.concatenate([a, b], 0)
            if masked:
                pair = jnp.where(row_live, pair, 0.0)
            left[:, start + g * 128:start + (g + 1) * 128] = pair.astype(BF16)

    def piece(columns, y, part, with_rows):
        @pl.loop(0, 4)
        def _(j):
            rows = pl.ds(pl.multiple_of(y * SLICE + j * 256, 256), 256)
            value = lax.dot_general(
                left[:, columns], wcat[rows, columns], NT, preferred_element_type=F32
            ).astype(BF16)
            part[y, :, pl.ds(pl.multiple_of(j * 256, 256), 256)] = value
            if with_rows:
                term = value.astype(F32) * (states[:, rows].astype(F32) * gains[:, rows])
                rterm[...] += term[:, :128] + term[:, 128:]

    def rs_copy(n, part, far, into, send, recv):
        src, dst, y = [
            (part.at[y_far, top], far.at[0], y_r),
            (part.at[y_far, bottom], far.at[1], y_l),
            (part.at[y_r, bottom], into.at[0, bottom], y_r),
            (part.at[y_r, top], into.at[0, top], y_r),
            (part.at[y_l, top], into.at[1, top], y_l),
            (part.at[y_l, bottom], into.at[1, bottom], y_l),
        ][n]
        return remote(src, dst, send.at[n], recv.at[n], at_y(y))

    def rs_recv(n, part, far, into, send, recv):
        dst = [
            far.at[0], far.at[1], into.at[0, bottom], into.at[0, top],
            into.at[1, top], into.at[1, bottom],
        ][n]
        remote(dst, dst, send.at[n], recv.at[n], at_y(y_r)).wait_recv()

    def rs_begin(columns, with_rows, args):
        part = args[0]
        piece(columns, y_far, part, with_rows)
        rs_copy(0, *args).start()
        rs_copy(1, *args).start()
        piece(columns, y_r, part, with_rows)
        rs_copy(2, *args).start()
        piece(columns, y_l, part, with_rows)
        rs_copy(4, *args).start()
        piece(columns, mp, part, with_rows)

    def rs_middle(args):
        part, far = args[:2]
        rs_recv(0, *args)
        part[y_r, top] = (part[y_r, top].astype(F32) + far[0].astype(F32)).astype(BF16)
        rs_copy(3, *args).start()
        rs_recv(1, *args)
        part[y_l, bottom] = (part[y_l, bottom].astype(F32) + far[1].astype(F32)).astype(BF16)
        rs_copy(5, *args).start()

    def rs_wait(args):
        for n in (2, 4, 3, 5):
            rs_recv(n, *args)

    l_args = (lpart, lfar, lin, l_s, l_r)
    g_args = (gpart, gfar, gin, rs_s, rs_r)
    first, second = pl.ds(0, GROUP), pl.ds(GROUP, GROUP)

    @pl.when(seg == 1)
    def _():
        for n in (1, 3):
            cot_recv(n)

        def gather_product(k):
            c = lax.rem(y_far + k, 4)
            rows = pl.ds(pl.multiple_of(c * SLICE, SLICE), SLICE)
            acc[:, GROUP:] += jnp.dot(cot[c], wcat[rows, GROUP:], preferred_element_type=F32)

        pl.loop(1, 4)(gather_product)
        for n in (4, 5):
            cot_recv(n)
        gather_product(0)

        for g in range(4):
            pair = jnp.where(row_live, acc[:, GROUP + g * 128:GROUP + (g + 1) * 128], 0.0)
            even, odd = exchange(pair[:HALF], pair[HALF:])
            dsend[2 * g] = even.astype(BF16)
            dsend[2 * g + 1] = odd.astype(BF16)
        for k in range(1, 8):
            d_copy(lax.rem(me + k, 8)).start()
        d_own.start()
        collect(obuf, o_r, o_own, GROUP, True)
        rs_begin(second, False, l_args)

    gacc[...] = jnp.zeros_like(gacc)

    def zg_copy(s):
        return remote(zout.at[s], zin.at[s], zg_s.at[s], zg_r.at[s], at_z(z_dn))

    @pl.loop(0, 4)
    def _(i):
        from_summary(dbuf, d_r, d_own, i)
        q0 = query(i)
        d0 = gradient(i)
        qd = q0 + d0
        delta = jnp.zeros((1, ROWS), F32)
        for j in range(4):
            dp = lax.dot_general(docs[i + j, :ROWS], d0, NT, preferred_element_type=F32)
            dpbuf[j] = dp
            delta = delta + jnp.sum(sbuf[i, j] * dp, axis=0, keepdims=True)
        out = jnp.zeros((128, ROWS), F32)
        low = low_half(ROWS)
        for j in range(4):
            ds = (sbuf[i, j] * (dpbuf[j] - delta)).astype(BF16)
            out = out + lax.dot_general(docs[i + j, :ROWS], ds, TN, preferred_element_type=F32)
            gk = jnp.dot(ds, qd, preferred_element_type=F32)
            gv = jnp.dot(pbuf[i, j], qd, preferred_element_type=F32)
            gacc[i + j] += jnp.where(low, SCALE * gk, gv)
        out = (SCALE * out).T
        dqsend[i] = jnp.where(
            low_half(HALF), out[:HALF], pltpu.roll(out[HALF:], 64, 1)
        ).astype(BF16)

        @pl.when(me != 4 + i)
        def _():
            dq_copy(i).start()

        @pl.when(me == 4 + i)
        def _():
            dq_own(i).start()

        @pl.when(i < 3)
        def _():
            zout[i] = gacc[i].astype(BF16)
            zg_copy(i).start()

    def g_copy(j):
        return remote(gout.at[j], gbuf.at[me], g_s.at[j], g_r.at[me], peer(j))

    def g_own(j):
        return pltpu.make_async_copy(gout.at[j], gbuf.at[me], loc_sem.at[2])

    for j in range(4):
        total = gacc[3 + j]
        if j > 0:
            remote(zin.at[j - 1], zin.at[j - 1], zg_s.at[0], zg_r.at[j - 1], at_z(z_up)).wait_recv()
            total = total + zin[j - 1].astype(F32)
        gout[j] = total.astype(BF16)

        @pl.when(me != j)
        def _():
            g_copy(j).start()

        @pl.when(me == j)
        def _():
            g_own(j).start()

    rterm[...] = jnp.zeros_like(rterm)

    @pl.when(seg == 1)
    def _():
        rs_middle(l_args)
        collect(dqbuf, dq_r, dq_own, 0, False)
        rs_begin(first, True, g_args)

    @pl.when(seg == 0)
    def _():
        for h in range(8):
            @pl.when(me == h)
            def _():
                g_own(quad).wait()

            @pl.when(me != h)
            def _():
                remote(gbuf.at[h], gbuf.at[h], g_r.at[h], g_r.at[h], peer(h)).wait_recv()
        for g in range(4):
            a, b = exchange(gbuf[2 * g].astype(F32), gbuf[2 * g + 1].astype(F32))
            left[:, g * 128:(g + 1) * 128] = a.astype(BF16)
            left[:, GROUP + g * 128:GROUP + (g + 1) * 128] = b.astype(BF16)
        rs_begin(pl.ds(0, 2 * GROUP), True, g_args)

    rsend[...] = jnp.broadcast_to(jnp.sum(rterm[...].T, axis=0, keepdims=True), (8, ROWS))

    def rt_copy(n, y):
        return remote(rsend, rin.at[n], rt_s.at[n], rt_r.at[n], at_y(y))

    for n, y in enumerate((y_r, y_l, y_far)):
        rt_copy(n, y).start()

    rs_middle(g_args)

    layer_out = pltpu.make_async_copy(lout, seg_hbm.at[0], out_sem.at[0])

    @pl.when(seg == 1)
    def _():
        rs_wait(l_args)

        @pl.loop(0, 8)
        def _(i):
            rows = pl.ds(pl.multiple_of(i * 32, 32), 32)
            value = lpart[mp, rows].astype(F32) + lin[0, rows].astype(F32) + lin[1, rows].astype(F32)
            lout[rows] = value.astype(BF16)

        layer_out.start()

    for n in range(3):
        remote(rin.at[n], rin.at[n], rt_s.at[n], rt_r.at[n], at_y(y_r)).wait_recv()
    sums = (rsend[...] + rin[0]) + (rin[1] + rin[2])
    rterm[...] = jnp.broadcast_to(sums[:1], (128, ROWS)).T

    rs_wait(g_args)

    @pl.loop(0, 8)
    def _(i):
        rows = pl.ds(pl.multiple_of(i * 32, 32), 32)
        value = gpart[mp, rows].astype(F32) + gin[0, rows].astype(F32) + gin[1, rows].astype(F32)
        inverse = rspread[rows]
        factor = rterm[rows] * (inverse * inverse * inverse) * (1.0 / WIDTH)
        gain = gains[:, own_columns]
        x = states[rows, own_columns].astype(F32)
        gfin[rows] = (gain * value * inverse[:, :1] - x * factor[:, :1]).astype(BF16)

    grad_out = pltpu.make_async_copy(gfin, grad_hbm.at[0], out_sem.at[1])
    grad_out.start()

    @pl.when(seg == 0)
    def _():
        normed_out.wait()
        for k in range(1, 8):
            kv_copy(lax.rem(me + k, 8)).wait_send()

    @pl.when(seg == 1)
    def _():
        layer_out.wait()
        for n in range(6):
            cot_copy(n).wait_send()
            rs_copy(n, *l_args).wait_send()
        for k in range(1, 8):
            q_copy(lax.rem(me + k, 8)).wait_send()
            d_copy(lax.rem(me + k, 8)).wait_send()

    for s in range(3):
        z_copy(s).wait_send()
        zg_copy(s).wait_send()
    for i in range(4):
        @pl.when(me != 4 + i)
        def _():
            o_copy(i).wait_send()
            dq_copy(i).wait_send()

        @pl.when(me != i)
        def _():
            g_copy(i).wait_send()
    for n in range(6):
        rs_copy(n, *g_args).wait_send()
    for n, y in enumerate((y_r, y_l, y_far)):
        rt_copy(n, y).wait_send()
    grad_out.wait()


def deliver(seg_in, grad_in, seg_out, grad_out):
    seg_out[...] = seg_in[...]
    grad_out[...] = grad_in[...]


def per_device(segment_in, norm_gains, projections, live_counts, cotangent):
    dma = lambda n: pltpu.SemaphoreType.DMA((n,))
    vmem = pltpu.VMEM
    shape = jax.ShapeDtypeStruct((1, ROWS, SLICE), BF16)
    hbm = pl.BlockSpec(memory_space=pl.ANY)
    half = pl.BlockSpec((1, HALF, SLICE), lambda i: (0, i, 0))
    results = pl.pallas_call(
        kernel,
        name="window_attention",
        out_shape=(shape, shape),
        in_specs=[pl.BlockSpec(memory_space=pltpu.SMEM)] + [hbm] * 4,
        out_specs=(hbm, hbm),
        scratch_shapes=[
            vmem((ROWS, WIDTH), BF16),
            vmem((1, WIDTH), F32),
            vmem((ROWS, WIDTH), BF16),
            vmem((ROWS, 128), F32),
            vmem((WIDTH, 2, GROUP), BF16),
            vmem((WIDTH, 2 * GROUP), BF16),
            vmem((ROWS, 2 * GROUP), F32),
            vmem((4, ROWS, SLICE), BF16),
            vmem((8, SLAB, 128), BF16),
            vmem((8, HALF, 128), BF16),
            vmem((8, HALF, 128), BF16),
            vmem((7, SLAB, 128), BF16),
            vmem((4, HALF, 128), BF16),
            vmem((4, HALF, 128), BF16),
            vmem((4, 4, ROWS, ROWS), F32),
            vmem((4, 4, ROWS, ROWS), BF16),
            vmem((4, ROWS, ROWS), F32),
            vmem((7, ROWS, 128), F32),
            vmem((4, HALF, 128), BF16),
            vmem((4, HALF, 128), BF16),
            vmem((8, HALF, 128), BF16),
            vmem((8, HALF, 128), BF16),
            vmem((3, ROWS, 128), BF16),
            vmem((3, ROWS, 128), BF16),
            vmem((4, ROWS, 128), BF16),
            vmem((8, ROWS, 128), BF16),
            vmem((ROWS, 2 * GROUP), BF16),
            vmem((4, ROWS, SLICE), BF16),
            vmem((2, HALF, SLICE), BF16),
            vmem((2, ROWS, SLICE), BF16),
            vmem((4, ROWS, SLICE), BF16),
            vmem((2, HALF, SLICE), BF16),
            vmem((2, ROWS, SLICE), BF16),
            vmem((ROWS, 128), F32),
            vmem((8, ROWS), F32),
            vmem((3, 8, ROWS), F32),
            vmem((ROWS, SLICE), BF16),
            vmem((ROWS, SLICE), BF16),
            dma(3), dma(4), dma(4), dma(2),
            dma(6), dma(6), dma(8), dma(7), dma(8), dma(4), dma(8), dma(4), dma(3), dma(3),
            dma(4), dma(8), dma(4), dma(8), dma(3), dma(3), dma(4), dma(8),
            dma(6), dma(6), dma(6), dma(6), dma(3), dma(3),
        ],
        compiler_params=pltpu.CompilerParams(
            collective_id=0, has_side_effects=True, vmem_limit_bytes=56 * 1024 * 1024
        ),
        cost_estimate=pl.CostEstimate(flops=10**10, bytes_accessed=12 * 2**20, transcendentals=2**20),
    )(live_counts.reshape(1, 2), segment_in, norm_gains, projections, cotangent)
    return pl.pallas_call(
        deliver,
        name="deliver",
        out_shape=(shape, shape),
        grid=(2,),
        in_specs=[half] * 2,
        out_specs=(half, half),
    )(*results)


def solution(mesh):
    in_specs = (
        P("segment", "blk", None),
        P("segment", None),
        P("segment", None, None, "mp"),
        P(None, "blk"),
        P("blk", "mp"),
    )
    out_specs = (P("segment", "blk", "mp"), P("segment", "blk", "mp"))
    return jax.shard_map(
        per_device, mesh=mesh, in_specs=in_specs, out_specs=out_specs, check_vma=False
    )
```

```python
import jax
import jax.numpy as jnp
from jax import lax
from jax.experimental import pallas as pl
from jax.experimental.pallas import tpu as pltpu
from jax.sharding import PartitionSpec as P

MESH = pl.DeviceIdType.MESH
F32 = jnp.float32
BF16 = jnp.bfloat16
EPSILON = 1e-06
SCALE = 0.125
NEGATIVE = -1e30
NT = (((1,), (1,)), ((), ()))
TN = (((0,), (0,)), ((), ()))
ROWS = 256
HALF = 128
WIDTH = 4096
SLICE = 1024
GROUP = 512
SLAB = ROWS + 16


def kernel(
    live_ref, x_hbm, gain_hbm, w_hbm, cot_hbm,
    seg_hbm, grad_hbm,
    states, gains, normed, rspread, wraw, wcat, acc, cot,
    kvsend, qsend, dsend, docs, qbuf, dbuf,
    sbuf, pbuf, dpbuf, gacc, osend, dqsend, obuf, dqbuf,
    zout, zin, gout, gbuf,
    left, lpart, lfar, lin, gpart, gfar, gin,
    rterm, rsend, rin, lout, gfin,
    load_sem, w_sem, loc_sem, out_sem,
    cot_s, cot_r, kv_s, doc_r, q_s, q_r, d_s, d_r, z_s, z_r,
    o_s, o_r, dq_s, dq_r, zg_s, zg_r, g_s, g_r,
    l_s, l_r, rs_s, rs_r, rt_s, rt_r,
):
    seg = lax.axis_index("segment")
    blk = lax.axis_index("blk")
    mp = lax.axis_index("mp")
    z = blk // 4
    quad = lax.rem(blk, 4)
    me = seg * 4 + quad
    n_z = lax.axis_size("blk") // 4
    z_up = lax.rem(z + 1, n_z)
    z_dn = lax.rem(z + n_z - 1, n_z)
    y_r, y_l, y_far = lax.rem(mp + 1, 4), lax.rem(mp + 3, 4), lax.rem(mp + 2, 4)

    def peer(t):
        return (t // 4, z * 4 + lax.rem(t, 4), mp)

    def at_y(y):
        return (seg, blk, y)

    def at_z(zz):
        return (seg, zz * 4 + quad, mp)

    def remote(src, dst, send, recv, to):
        return pltpu.make_async_remote_copy(
            src_ref=src, dst_ref=dst, send_sem=send, recv_sem=recv,
            device_id=to, device_id_type=MESH,
        )

    x_load = pltpu.make_async_copy(x_hbm.at[0], states, load_sem.at[0])
    g_load = pltpu.make_async_copy(gain_hbm, gains, load_sem.at[1])
    c_load = pltpu.make_async_copy(cot_hbm, cot.at[mp], load_sem.at[2])
    x_load.start()
    g_load.start()

    @pl.when(seg == 1)
    def _():
        c_load.start()

    def w_load(c):
        rows = pl.ds(pl.multiple_of(c * SLICE, SLICE), SLICE)
        return pltpu.make_async_copy(w_hbm.at[0, rows], wraw.at[rows], w_sem.at[c])

    for c in range(4):
        w_load(c).start()

    barrier = pltpu.get_barrier_semaphore()
    for k in range(1, 8):
        pl.semaphore_signal(barrier, inc=1, device_id=peer(lax.rem(me + k, 8)), device_id_type=MESH)
    for to in (at_y(y_r), at_y(y_l), at_y(y_far), at_z(z_up), at_z(z_dn)):
        pl.semaphore_signal(barrier, inc=1, device_id=to, device_id_type=MESH)

    top, bottom = pl.ds(0, HALF), pl.ds(HALF, HALF)

    def cot_copy(n):
        own_r = lambda h: (cot.at[mp, h], at_y(y_r))
        own_l = lambda h: (cot.at[mp, h], at_y(y_l))
        ref, to = [
            own_r(top), own_r(bottom), own_l(bottom), own_l(top),
            (cot.at[y_l, top], at_y(y_r)), (cot.at[y_r, bottom], at_y(y_l)),
        ][n]
        return remote(ref, ref, cot_s.at[n], cot_r.at[n], to)

    def cot_recv(n):
        ref = [
            cot.at[y_l, top], cot.at[y_l, bottom], cot.at[y_r, bottom], cot.at[y_r, top],
            cot.at[y_far, top], cot.at[y_far, bottom],
        ][n]
        remote(ref, ref, cot_s.at[n], cot_r.at[n], at_y(y_r)).wait_recv()

    def norm(i):
        rows = pl.ds(pl.multiple_of(i * 32, 32), 32)
        x = states[rows].astype(F32)
        inverse = 1.0 / jnp.sqrt(jnp.mean(x * x, axis=-1, keepdims=True) + EPSILON)
        rspread[rows] = jnp.broadcast_to(inverse, (32, 128))
        normed[rows] = (x * inverse * gains[...]).astype(BF16)

    x_load.wait()
    g_load.wait()
    pl.loop(0, 4)(norm)

    @pl.when(seg == 1)
    def _():
        pl.semaphore_wait(barrier, 12)
        c_load.wait()
        for n in (0, 2):
            cot_copy(n).start()

    pl.loop(4, 8)(norm)

    own_columns = pl.ds(pl.multiple_of(mp * SLICE, SLICE), SLICE)
    normed_out = pltpu.make_async_copy(normed.at[:, own_columns], seg_hbm.at[0], out_sem.at[0])

    @pl.when(seg == 0)
    def _():
        normed_out.start()

    def low_half(rows):
        return lax.broadcasted_iota(jnp.int32, (rows, 128), 1) < 64

    def exchange(a, b):
        low = low_half(a.shape[0])
        return jnp.where(low, a, pltpu.roll(b, 64, 1)), jnp.where(low, pltpu.roll(a, 64, 1), b)

    row_live = lax.broadcasted_iota(jnp.int32, (ROWS, 128), 0) < live_ref[0, 1]

    def kv_copy(t):
        return remote(kvsend.at[t], docs.at[3 + quad], kv_s.at[t], doc_r.at[3 + quad], peer(t))

    def q_copy(t):
        return remote(qsend.at[t], qbuf.at[quad], q_s.at[t], q_r.at[quad], peer(t))

    def d_copy(t):
        return remote(dsend.at[t], dbuf.at[quad], d_s.at[t], d_r.at[quad], peer(t))

    kv_own = pltpu.make_async_copy(kvsend.at[me], docs.at[3 + quad], loc_sem.at[0])
    q_own = pltpu.make_async_copy(qsend.at[me], qbuf.at[quad], loc_sem.at[0])
    d_own = pltpu.make_async_copy(dsend.at[me], dbuf.at[quad], loc_sem.at[1])

    def spread_weights(c):
        w_load(c).wait()

        @pl.loop(0, 4)
        def _(j):
            rows = pl.ds(pl.multiple_of(c * SLICE + j * 256, 256), 256)
            wcat[rows] = wraw[rows].reshape(256, 2 * GROUP)

    @pl.when(seg == 0)
    def _():
        pl.loop(0, 4)(spread_weights)
        pl.semaphore_wait(barrier, 12)
        count = jnp.full((16, 128), live_ref[0, 0], jnp.int32).astype(F32).astype(BF16)
        for stage in (1, 0):
            start = stage * 256
            keys = jnp.dot(normed[...], wcat[:, start:start + 256], preferred_element_type=F32)
            start = GROUP + start
            values = jnp.dot(normed[...], wcat[:, start:start + 256], preferred_element_type=F32)
            for g in range(2):
                part = slice(g * 128, (g + 1) * 128)
                for k, slab in enumerate(exchange(keys[:, part], values[:, part])):
                    t = 4 * stage + 2 * g + k
                    kvsend[t, :ROWS] = slab.astype(BF16)
                    kvsend[t, ROWS:] = count
            for k in range(4):
                t = 4 * stage + lax.rem(quad + k, 4)
                if stage == 0 and k == 0:
                    kv_own.start()
                else:
                    kv_copy(t).start()

    @pl.when(seg == 1)
    def _():
        acc[...] = jnp.zeros_like(acc)

        @pl.loop(0, 4)
        def _(c):
            spread_weights(c)
            rows = pl.ds(pl.multiple_of(c * SLICE, SLICE), SLICE)
            acc[:, :GROUP] += jnp.dot(
                normed[:, rows], wcat[rows, :GROUP], preferred_element_type=F32
            )

        for g in range(4):
            pair = acc[:, g * 128:(g + 1) * 128]
            even, odd = exchange(pair[:HALF], pair[HALF:])
            qsend[2 * g] = even.astype(BF16)
            qsend[2 * g + 1] = odd.astype(BF16)
        for k in range(1, 8):
            q_copy(lax.rem(me + k, 8)).start()
        q_own.start()
        cot_recv(0)
        cot_recv(2)
        for n in (1, 3, 4, 5):
            cot_copy(n).start()

    def z_copy(s):
        return remote(docs.at[s + 4], docs.at[s], z_s.at[s], z_r.at[s], at_z(z_up))

    def z_recv(s):
        remote(docs.at[s], docs.at[s], z_s.at[s], z_r.at[s], at_z(z_up)).wait_recv()

    for j in (3, 2, 1, 0):
        @pl.when(me == j)
        def _():
            kv_own.wait()

        @pl.when(me != j)
        def _():
            remote(docs.at[3 + j], docs.at[3 + j], kv_s.at[0], doc_r.at[3 + j], peer(j)).wait_recv()

        if j > 0:
            z_copy(j - 1).start()

    def from_summary(buf, recv, own, i):
        @pl.when(me == 4 + i)
        def _():
            own.wait()

        @pl.when(me != 4 + i)
        def _():
            remote(buf.at[i], buf.at[i], recv.at[i], recv.at[i], peer(4 + i)).wait_recv()

    def query(i):
        slab = qbuf[i].astype(F32)
        low = low_half(HALF)
        a = jnp.where(low, slab, 0.0)
        b = jnp.where(low, pltpu.roll(slab, 64, 1), 0.0)
        return jnp.concatenate([a, b], 0).astype(BF16)

    def gradient(i):
        slab = dbuf[i].astype(F32)
        low = low_half(HALF)
        a = jnp.where(low, 0.0, pltpu.roll(slab, 64, 1))
        b = jnp.where(low, 0.0, slab)
        return jnp.concatenate([a, b], 0).astype(BF16)

    def o_copy(i):
        return remote(osend.at[i], obuf.at[me], o_s.at[i], o_r.at[me], peer(4 + i))

    def dq_copy(i):
        return remote(dqsend.at[i], dqbuf.at[me], dq_s.at[i], dq_r.at[me], peer(4 + i))

    def o_own(i):
        return pltpu.make_async_copy(osend.at[i], obuf.at[me], loc_sem.at[2])

    def dq_own(i):
        return pltpu.make_async_copy(dqsend.at[i], dqbuf.at[me], loc_sem.at[3])

    @pl.loop(0, 4)
    def _(n):
        i = 3 - n

        @pl.when(i < 3)
        def _():
            z_recv(i)

        from_summary(qbuf, q_r, q_own, i)
        q0 = query(i)
        position = lax.broadcasted_iota(jnp.int32, (ROWS, ROWS), 0).astype(F32)
        peak = jnp.full((1, ROWS), NEGATIVE, F32)
        for j in range(4):
            s = lax.dot_general(docs[i + j, :ROWS], q0, NT, preferred_element_type=F32) * SCALE
            count = docs[i + j, ROWS:].astype(F32)[:1]
            count = jnp.where(4 * z - 3 + i + j >= 0, count, 0.0)
            count = jnp.concatenate([count, count], 1)
            s = jnp.where(position < count, s, NEGATIVE)
            sbuf[i, j] = s
            peak = jnp.maximum(peak, jnp.max(s, axis=0, keepdims=True))
        total = jnp.zeros((1, ROWS), F32)
        for j in range(4):
            e = jnp.exp(sbuf[i, j] - peak)
            sbuf[i, j] = e
            total = total + jnp.sum(e, axis=0, keepdims=True)
        share = 1.0 / total
        out = jnp.zeros((128, ROWS), F32)
        for j in range(4):
            probs = sbuf[i, j] * share
            sbuf[i, j] = probs
            low = probs.astype(BF16)
            pbuf[i, j] = low
            out = out + lax.dot_general(docs[i + j, :ROWS], low, TN, preferred_element_type=F32)
        out = out.T
        osend[i] = jnp.where(
            low_half(HALF), pltpu.roll(out[:HALF], 64, 1), out[HALF:]
        ).astype(BF16)

        @pl.when(me != 4 + i)
        def _():
            o_copy(i).start()

        @pl.when(me == 4 + i)
        def _():
            o_own(i).start()

    def collect(buf, recv, own, start, masked):
        for h in range(8):
            @pl.when(me == h)
            def _():
                own(quad).wait()

            @pl.when(me != h)
            def _():
                remote(buf.at[h], buf.at[h], recv.at[h], recv.at[h], peer(h)).wait_recv()
        for g in range(4):
            a, b = exchange(buf[2 * g].astype(F32), buf[2 * g + 1].astype(F32))
            pair = jnp.concatenate([a, b], 0)
            if masked:
                pair = jnp.where(row_live, pair, 0.0)
            left[:, start + g * 128:start + (g + 1) * 128] = pair.astype(BF16)

    def piece(columns, y, part):
        rows = pl.ds(pl.multiple_of(y * SLICE, SLICE), SLICE)
        part[y] = lax.dot_general(
            left[:, columns], wcat[rows, columns], NT, preferred_element_type=F32
        ).astype(BF16)

    def row_terms(y, part):
        @pl.loop(0, 4)
        def _(j):
            rows = pl.ds(pl.multiple_of(y * SLICE + j * 256, 256), 256)
            value = part[y, :, pl.ds(pl.multiple_of(j * 256, 256), 256)]
            term = value.astype(F32) * (states[:, rows].astype(F32) * gains[:, rows])
            rterm[...] += term[:, :128] + term[:, 128:]

    def rs_copy(n, part, far, into, send, recv):
        src, dst, y = [
            (part.at[y_far, top], far.at[0], y_r),
            (part.at[y_far, bottom], far.at[1], y_l),
            (part.at[y_r, bottom], into.at[0, bottom], y_r),
            (part.at[y_r, top], into.at[0, top], y_r),
            (part.at[y_l, top], into.at[1, top], y_l),
            (part.at[y_l, bottom], into.at[1, bottom], y_l),
        ][n]
        return remote(src, dst, send.at[n], recv.at[n], at_y(y))

    def rs_recv(n, part, far, into, send, recv):
        dst = [
            far.at[0], far.at[1], into.at[0, bottom], into.at[0, top],
            into.at[1, top], into.at[1, bottom],
        ][n]
        remote(dst, dst, send.at[n], recv.at[n], at_y(y_r)).wait_recv()

    def rs_begin(columns, with_rows, args):
        part = args[0]
        piece(columns, y_far, part)
        rs_copy(0, *args).start()
        rs_copy(1, *args).start()
        piece(columns, y_r, part)
        rs_copy(2, *args).start()
        piece(columns, y_l, part)
        rs_copy(4, *args).start()
        piece(columns, mp, part)
        if with_rows:
            for y in (y_far, y_r, y_l, mp):
                row_terms(y, part)

    def rs_middle(args):
        part, far = args[:2]
        rs_recv(0, *args)
        part[y_r, top] = (part[y_r, top].astype(F32) + far[0].astype(F32)).astype(BF16)
        rs_copy(3, *args).start()
        rs_recv(1, *args)
        part[y_l, bottom] = (part[y_l, bottom].astype(F32) + far[1].astype(F32)).astype(BF16)
        rs_copy(5, *args).start()

    def rs_wait(args):
        for n in (2, 4, 3, 5):
            rs_recv(n, *args)

    l_args = (lpart, lfar, lin, l_s, l_r)
    g_args = (gpart, gfar, gin, rs_s, rs_r)
    first, second = pl.ds(0, GROUP), pl.ds(GROUP, GROUP)

    @pl.when(seg == 1)
    def _():
        for n in (1, 3):
            cot_recv(n)

        def gather_product(k):
            c = lax.rem(y_far + k, 4)
            rows = pl.ds(pl.multiple_of(c * SLICE, SLICE), SLICE)
            acc[:, GROUP:] += jnp.dot(cot[c], wcat[rows, GROUP:], preferred_element_type=F32)

        pl.loop(1, 4)(gather_product)
        for n in (4, 5):
            cot_recv(n)
        gather_product(0)

        for g in range(4):
            pair = jnp.where(row_live, acc[:, GROUP + g * 128:GROUP + (g + 1) * 128], 0.0)
            even, odd = exchange(pair[:HALF], pair[HALF:])
            dsend[2 * g] = even.astype(BF16)
            dsend[2 * g + 1] = odd.astype(BF16)
        for k in range(1, 8):
            d_copy(lax.rem(me + k, 8)).start()
        d_own.start()
        collect(obuf, o_r, o_own, GROUP, True)
        rs_begin(second, False, l_args)

    gacc[...] = jnp.zeros_like(gacc)

    def zg_copy(s):
        return remote(zout.at[s], zin.at[s], zg_s.at[s], zg_r.at[s], at_z(z_dn))

    for i in range(4):
        from_summary(dbuf, d_r, d_own, i)

    for i in range(4):
        q0 = query(i)
        d0 = gradient(i)
        qd = q0 + d0
        delta = jnp.zeros((1, ROWS), F32)
        for j in range(4):
            dp = lax.dot_general(docs[i + j, :ROWS], d0, NT, preferred_element_type=F32)
            dpbuf[i % 2, j] = dp
            delta = delta + jnp.sum(sbuf[i, j] * dp, axis=0, keepdims=True)
        out = jnp.zeros((128, ROWS), F32)
        low = low_half(ROWS)
        for j in range(4):
            ds = (sbuf[i, j] * (dpbuf[i % 2, j] - delta)).astype(BF16)
            out = out + lax.dot_general(docs[i + j, :ROWS], ds, TN, preferred_element_type=F32)
            gk = jnp.dot(ds, qd, preferred_element_type=F32)
            gv = jnp.dot(pbuf[i, j], qd, preferred_element_type=F32)
            gacc[i + j] += jnp.where(low, SCALE * gk, gv)
        out = (SCALE * out).T
        dqsend[i] = jnp.where(
            low_half(HALF), out[:HALF], pltpu.roll(out[HALF:], 64, 1)
        ).astype(BF16)
        if i < 3:
            zout[i] = gacc[i].astype(BF16)
            zg_copy(i).start()

    for i in range(4):
        @pl.when(me != 4 + i)
        def _():
            dq_copy(i).start()

        @pl.when(me == 4 + i)
        def _():
            dq_own(i).start()

    def g_copy(j):
        return remote(gout.at[j], gbuf.at[me], g_s.at[j], g_r.at[me], peer(j))

    def g_own(j):
        return pltpu.make_async_copy(gout.at[j], gbuf.at[me], loc_sem.at[2])

    for j in range(4):
        total = gacc[3 + j]
        if j > 0:
            remote(zin.at[j - 1], zin.at[j - 1], zg_s.at[0], zg_r.at[j - 1], at_z(z_up)).wait_recv()
            total = total + zin[j - 1].astype(F32)
        gout[j] = total.astype(BF16)

        @pl.when(me != j)
        def _():
            g_copy(j).start()

        @pl.when(me == j)
        def _():
            g_own(j).start()

    rterm[...] = jnp.zeros_like(rterm)

    @pl.when(seg == 1)
    def _():
        rs_middle(l_args)
        collect(dqbuf, dq_r, dq_own, 0, False)
        rs_begin(first, True, g_args)

    @pl.when(seg == 0)
    def _():
        for h in range(8):
            @pl.when(me == h)
            def _():
                g_own(quad).wait()

            @pl.when(me != h)
            def _():
                remote(gbuf.at[h], gbuf.at[h], g_r.at[h], g_r.at[h], peer(h)).wait_recv()
        for g in range(4):
            a, b = exchange(gbuf[2 * g].astype(F32), gbuf[2 * g + 1].astype(F32))
            left[:, g * 128:(g + 1) * 128] = a.astype(BF16)
            left[:, GROUP + g * 128:GROUP + (g + 1) * 128] = b.astype(BF16)
        rs_begin(pl.ds(0, 2 * GROUP), True, g_args)

    rsend[...] = jnp.broadcast_to(jnp.sum(rterm[...].T, axis=0, keepdims=True), (8, ROWS))

    def rt_copy(n, y):
        return remote(rsend, rin.at[n], rt_s.at[n], rt_r.at[n], at_y(y))

    for n, y in enumerate((y_r, y_l, y_far)):
        rt_copy(n, y).start()

    rs_middle(g_args)

    layer_out = pltpu.make_async_copy(lout, seg_hbm.at[0], out_sem.at[0])

    @pl.when(seg == 1)
    def _():
        rs_wait(l_args)

        @pl.loop(0, 8)
        def _(i):
            rows = pl.ds(pl.multiple_of(i * 32, 32), 32)
            value = lpart[mp, rows].astype(F32) + lin[0, rows].astype(F32) + lin[1, rows].astype(F32)
            lout[rows] = value.astype(BF16)

        layer_out.start()

    for n in range(3):
        remote(rin.at[n], rin.at[n], rt_s.at[n], rt_r.at[n], at_y(y_r)).wait_recv()
    sums = (rsend[...] + rin[0]) + (rin[1] + rin[2])
    rterm[...] = jnp.broadcast_to(sums[:1], (128, ROWS)).T

    rs_wait(g_args)

    @pl.loop(0, 8)
    def _(i):
        rows = pl.ds(pl.multiple_of(i * 32, 32), 32)
        value = gpart[mp, rows].astype(F32) + gin[0, rows].astype(F32) + gin[1, rows].astype(F32)
        inverse = rspread[rows]
        factor = rterm[rows] * (inverse * inverse * inverse) * (1.0 / WIDTH)
        gain = gains[:, own_columns]
        x = states[rows, own_columns].astype(F32)
        gfin[rows] = (gain * value * inverse[:, :1] - x * factor[:, :1]).astype(BF16)

    grad_out = pltpu.make_async_copy(gfin, grad_hbm.at[0], out_sem.at[1])
    grad_out.start()

    @pl.when(seg == 0)
    def _():
        normed_out.wait()
        for k in range(1, 8):
            kv_copy(lax.rem(me + k, 8)).wait_send()

    @pl.when(seg == 1)
    def _():
        layer_out.wait()
        for n in range(6):
            cot_copy(n).wait_send()
            rs_copy(n, *l_args).wait_send()
        for k in range(1, 8):
            q_copy(lax.rem(me + k, 8)).wait_send()
            d_copy(lax.rem(me + k, 8)).wait_send()

    for s in range(3):
        z_copy(s).wait_send()
        zg_copy(s).wait_send()
    for i in range(4):
        @pl.when(me != 4 + i)
        def _():
            o_copy(i).wait_send()
            dq_copy(i).wait_send()

        @pl.when(me != i)
        def _():
            g_copy(i).wait_send()
    for n in range(6):
        rs_copy(n, *g_args).wait_send()
    for n, y in enumerate((y_r, y_l, y_far)):
        rt_copy(n, y).wait_send()
    grad_out.wait()


def deliver(seg_in, grad_in, seg_out, grad_out):
    seg_out[...] = seg_in[...]
    grad_out[...] = grad_in[...]


def per_device(segment_in, norm_gains, projections, live_counts, cotangent):
    dma = lambda n: pltpu.SemaphoreType.DMA((n,))
    vmem = pltpu.VMEM
    shape = jax.ShapeDtypeStruct((1, ROWS, SLICE), BF16)
    hbm = pl.BlockSpec(memory_space=pl.ANY)
    half = pl.BlockSpec((1, HALF, SLICE), lambda i: (0, i, 0))
    results = pl.pallas_call(
        kernel,
        name="window_attention",
        out_shape=(shape, shape),
        in_specs=[pl.BlockSpec(memory_space=pltpu.SMEM)] + [hbm] * 4,
        out_specs=(hbm, hbm),
        scratch_shapes=[
            vmem((ROWS, WIDTH), BF16),
            vmem((1, WIDTH), F32),
            vmem((ROWS, WIDTH), BF16),
            vmem((ROWS, 128), F32),
            vmem((WIDTH, 2, GROUP), BF16),
            vmem((WIDTH, 2 * GROUP), BF16),
            vmem((ROWS, 2 * GROUP), F32),
            vmem((4, ROWS, SLICE), BF16),
            vmem((8, SLAB, 128), BF16),
            vmem((8, HALF, 128), BF16),
            vmem((8, HALF, 128), BF16),
            vmem((7, SLAB, 128), BF16),
            vmem((4, HALF, 128), BF16),
            vmem((4, HALF, 128), BF16),
            vmem((4, 4, ROWS, ROWS), F32),
            vmem((4, 4, ROWS, ROWS), BF16),
            vmem((2, 4, ROWS, ROWS), F32),
            vmem((7, ROWS, 128), F32),
            vmem((4, HALF, 128), BF16),
            vmem((4, HALF, 128), BF16),
            vmem((8, HALF, 128), BF16),
            vmem((8, HALF, 128), BF16),
            vmem((3, ROWS, 128), BF16),
            vmem((3, ROWS, 128), BF16),
            vmem((4, ROWS, 128), BF16),
            vmem((8, ROWS, 128), BF16),
            vmem((ROWS, 2 * GROUP), BF16),
            vmem((4, ROWS, SLICE), BF16),
            vmem((2, HALF, SLICE), BF16),
            vmem((2, ROWS, SLICE), BF16),
            vmem((4, ROWS, SLICE), BF16),
            vmem((2, HALF, SLICE), BF16),
            vmem((2, ROWS, SLICE), BF16),
            vmem((ROWS, 128), F32),
            vmem((8, ROWS), F32),
            vmem((3, 8, ROWS), F32),
            vmem((ROWS, SLICE), BF16),
            vmem((ROWS, SLICE), BF16),
            dma(3), dma(4), dma(4), dma(2),
            dma(6), dma(6), dma(8), dma(7), dma(8), dma(4), dma(8), dma(4), dma(3), dma(3),
            dma(4), dma(8), dma(4), dma(8), dma(3), dma(3), dma(4), dma(8),
            dma(6), dma(6), dma(6), dma(6), dma(3), dma(3),
        ],
        compiler_params=pltpu.CompilerParams(
            collective_id=0, has_side_effects=True, vmem_limit_bytes=56 * 1024 * 1024
        ),
        cost_estimate=pl.CostEstimate(flops=10**10, bytes_accessed=12 * 2**20, transcendentals=2**20),
    )(live_counts.reshape(1, 2), segment_in, norm_gains, projections, cotangent)
    return pl.pallas_call(
        deliver,
        name="deliver",
        out_shape=(shape, shape),
        grid=(2,),
        in_specs=[half] * 2,
        out_specs=(half, half),
    )(*results)


def solution(mesh):
    in_specs = (
        P("segment", "blk", None),
        P("segment", None),
        P("segment", None, None, "mp"),
        P(None, "blk"),
        P("blk", "mp"),
    )
    out_specs = (P("segment", "blk", "mp"), P("segment", "blk", "mp"))
    return jax.shard_map(
        per_device, mesh=mesh, in_specs=in_specs, out_specs=out_specs, check_vma=False
    )
```

```python
import jax
import jax.numpy as jnp
from jax import lax
from jax.experimental import pallas as pl
from jax.experimental.pallas import tpu as pltpu
from jax.sharding import PartitionSpec as P

MESH = pl.DeviceIdType.MESH
F32 = jnp.float32
BF16 = jnp.bfloat16
EPSILON = 1e-06
SCALE = 0.125
NEGATIVE = -1e30
NT = (((1,), (1,)), ((), ()))
TN = (((0,), (0,)), ((), ()))
ROWS = 256
HALF = 128
WIDTH = 4096
SLICE = 1024
GROUP = 512
SLAB = ROWS + 16


def kernel(
    live_ref, x_hbm, gain_hbm, w_hbm, cot_hbm,
    seg_hbm, grad_hbm,
    states, gains, normed, rspread, wraw, wcat, acc, cot,
    kvsend, qsend, dsend, docs, qbuf, dbuf,
    sbuf, pbuf, dpbuf, gacc, osend, dqsend, obuf, dqbuf,
    zout, zin, gout, gbuf,
    left, lpart, lfar, lin, gpart, gfar, gin,
    rterm, rsend, rin, lout, gfin,
    load_sem, w_sem, loc_sem, out_sem,
    cot_s, cot_r, kv_s, doc_r, q_s, q_r, d_s, d_r, z_s, z_r,
    o_s, o_r, dq_s, dq_r, zg_s, zg_r, g_s, g_r,
    l_s, l_r, rs_s, rs_r, rt_s, rt_r,
):
    seg = lax.axis_index("segment")
    blk = lax.axis_index("blk")
    mp = lax.axis_index("mp")
    z = blk // 4
    quad = lax.rem(blk, 4)
    me = seg * 4 + quad
    n_z = lax.axis_size("blk") // 4
    z_up = lax.rem(z + 1, n_z)
    z_dn = lax.rem(z + n_z - 1, n_z)
    y_r, y_l, y_far = lax.rem(mp + 1, 4), lax.rem(mp + 3, 4), lax.rem(mp + 2, 4)

    def peer(t):
        return (t // 4, z * 4 + lax.rem(t, 4), mp)

    def at_y(y):
        return (seg, blk, y)

    def at_z(zz):
        return (seg, zz * 4 + quad, mp)

    def remote(src, dst, send, recv, to):
        return pltpu.make_async_remote_copy(
            src_ref=src, dst_ref=dst, send_sem=send, recv_sem=recv,
            device_id=to, device_id_type=MESH,
        )

    x_load = pltpu.make_async_copy(x_hbm.at[0], states, load_sem.at[0])
    g_load = pltpu.make_async_copy(gain_hbm, gains, load_sem.at[1])
    c_load = pltpu.make_async_copy(cot_hbm, cot.at[mp], load_sem.at[2])
    x_load.start()
    g_load.start()

    @pl.when(seg == 1)
    def _():
        c_load.start()

    def w_load(c):
        rows = pl.ds(pl.multiple_of(c * SLICE, SLICE), SLICE)
        return pltpu.make_async_copy(w_hbm.at[0, rows], wraw.at[rows], w_sem.at[c])

    for c in range(4):
        w_load(c).start()

    barrier = pltpu.get_barrier_semaphore()
    for k in range(1, 8):
        pl.semaphore_signal(barrier, inc=1, device_id=peer(lax.rem(me + k, 8)), device_id_type=MESH)
    for to in (at_y(y_r), at_y(y_l), at_y(y_far), at_z(z_up), at_z(z_dn)):
        pl.semaphore_signal(barrier, inc=1, device_id=to, device_id_type=MESH)

    top, bottom = pl.ds(0, HALF), pl.ds(HALF, HALF)

    def cot_copy(n):
        own_r = lambda h: (cot.at[mp, h], at_y(y_r))
        own_l = lambda h: (cot.at[mp, h], at_y(y_l))
        ref, to = [
            own_r(top), own_r(bottom), own_l(bottom), own_l(top),
            (cot.at[y_l, top], at_y(y_r)), (cot.at[y_r, bottom], at_y(y_l)),
        ][n]
        return remote(ref, ref, cot_s.at[n], cot_r.at[n], to)

    def cot_recv(n):
        ref = [
            cot.at[y_l, top], cot.at[y_l, bottom], cot.at[y_r, bottom], cot.at[y_r, top],
            cot.at[y_far, top], cot.at[y_far, bottom],
        ][n]
        remote(ref, ref, cot_s.at[n], cot_r.at[n], at_y(y_r)).wait_recv()

    def norm(i):
        rows = pl.ds(pl.multiple_of(i * 32, 32), 32)
        x = states[rows].astype(F32)
        inverse = 1.0 / jnp.sqrt(jnp.mean(x * x, axis=-1, keepdims=True) + EPSILON)
        rspread[rows] = jnp.broadcast_to(inverse, (32, 128))
        normed[rows] = (x * inverse * gains[...]).astype(BF16)

    x_load.wait()
    g_load.wait()
    pl.loop(0, 4)(norm)

    @pl.when(seg == 1)
    def _():
        pl.semaphore_wait(barrier, 12)
        c_load.wait()
        for n in (0, 2):
            cot_copy(n).start()

    pl.loop(4, 8)(norm)

    own_columns = pl.ds(pl.multiple_of(mp * SLICE, SLICE), SLICE)
    normed_out = pltpu.make_async_copy(normed.at[:, own_columns], seg_hbm.at[0], out_sem.at[0])

    @pl.when(seg == 0)
    def _():
        normed_out.start()

    def low_half(rows):
        return lax.broadcasted_iota(jnp.int32, (rows, 128), 1) < 64

    def exchange(a, b):
        low = low_half(a.shape[0])
        return jnp.where(low, a, pltpu.roll(b, 64, 1)), jnp.where(low, pltpu.roll(a, 64, 1), b)

    row_live = lax.broadcasted_iota(jnp.int32, (ROWS, 128), 0) < live_ref[0, 1]

    def kv_copy(t):
        return remote(kvsend.at[t], docs.at[3 + quad], kv_s.at[t], doc_r.at[3 + quad], peer(t))

    def q_copy(t):
        return remote(qsend.at[t], qbuf.at[quad], q_s.at[t], q_r.at[quad], peer(t))

    def d_copy(t):
        return remote(dsend.at[t], dbuf.at[quad], d_s.at[t], d_r.at[quad], peer(t))

    kv_own = pltpu.make_async_copy(kvsend.at[me], docs.at[3 + quad], loc_sem.at[0])
    q_own = pltpu.make_async_copy(qsend.at[me], qbuf.at[quad], loc_sem.at[0])
    d_own = pltpu.make_async_copy(dsend.at[me], dbuf.at[quad], loc_sem.at[1])

    def spread_weights(c):
        w_load(c).wait()

        @pl.loop(0, 4)
        def _(j):
            rows = pl.ds(pl.multiple_of(c * SLICE + j * 256, 256), 256)
            wcat[rows] = wraw[rows].reshape(256, 2 * GROUP)

    @pl.when(seg == 0)
    def _():
        pl.loop(0, 4)(spread_weights)
        pl.semaphore_wait(barrier, 12)
        count = jnp.full((16, 128), live_ref[0, 0], jnp.int32).astype(F32).astype(BF16)
        for stage in (1, 0):
            start = stage * 256
            keys = jnp.dot(normed[...], wcat[:, start:start + 256], preferred_element_type=F32)
            start = GROUP + start
            values = jnp.dot(normed[...], wcat[:, start:start + 256], preferred_element_type=F32)
            for g in range(2):
                part = slice(g * 128, (g + 1) * 128)
                for k, slab in enumerate(exchange(keys[:, part], values[:, part])):
                    t = 4 * stage + 2 * g + k
                    kvsend[t, :ROWS] = slab.astype(BF16)
                    kvsend[t, ROWS:] = count
            for k in range(4):
                t = 4 * stage + lax.rem(quad + k, 4)
                if stage == 0 and k == 0:
                    kv_own.start()
                else:
                    kv_copy(t).start()

    @pl.when(seg == 1)
    def _():
        acc[...] = jnp.zeros_like(acc)

        @pl.loop(0, 4)
        def _(c):
            spread_weights(c)
            rows = pl.ds(pl.multiple_of(c * SLICE, SLICE), SLICE)
            acc[:, :GROUP] += jnp.dot(
                normed[:, rows], wcat[rows, :GROUP], preferred_element_type=F32
            )

        for g in range(4):
            pair = acc[:, g * 128:(g + 1) * 128]
            even, odd = exchange(pair[:HALF], pair[HALF:])
            qsend[2 * g] = even.astype(BF16)
            qsend[2 * g + 1] = odd.astype(BF16)
        for k in range(1, 8):
            q_copy(lax.rem(me + k, 8)).start()
        q_own.start()
        cot_recv(0)
        cot_recv(2)
        for n in (1, 3, 4, 5):
            cot_copy(n).start()

    gacc[...] = jnp.zeros_like(gacc)
    rterm[...] = jnp.zeros_like(rterm)

    def z_copy(s):
        return remote(docs.at[s + 4], docs.at[s], z_s.at[s], z_r.at[s], at_z(z_up))

    def z_recv(s):
        remote(docs.at[s], docs.at[s], z_s.at[s], z_r.at[s], at_z(z_up)).wait_recv()

    for j in (3, 2, 1, 0):
        @pl.when(me == j)
        def _():
            kv_own.wait()

        @pl.when(me != j)
        def _():
            remote(docs.at[3 + j], docs.at[3 + j], kv_s.at[0], doc_r.at[3 + j], peer(j)).wait_recv()

        if j > 0:
            z_copy(j - 1).start()

    def from_summary(buf, recv, own, i):
        @pl.when(me == 4 + i)
        def _():
            own.wait()

        @pl.when(me != 4 + i)
        def _():
            remote(buf.at[i], buf.at[i], recv.at[i], recv.at[i], peer(4 + i)).wait_recv()

    def query(i):
        slab = qbuf[i].astype(F32)
        low = low_half(HALF)
        a = jnp.where(low, slab, 0.0)
        b = jnp.where(low, pltpu.roll(slab, 64, 1), 0.0)
        return jnp.concatenate([a, b], 0).astype(BF16)

    def gradient(i):
        slab = dbuf[i].astype(F32)
        low = low_half(HALF)
        a = jnp.where(low, 0.0, pltpu.roll(slab, 64, 1))
        b = jnp.where(low, 0.0, slab)
        return jnp.concatenate([a, b], 0).astype(BF16)

    def o_copy(i):
        return remote(osend.at[i], obuf.at[me], o_s.at[i], o_r.at[me], peer(4 + i))

    def dq_copy(i):
        return remote(dqsend.at[i], dqbuf.at[me], dq_s.at[i], dq_r.at[me], peer(4 + i))

    def o_own(i):
        return pltpu.make_async_copy(osend.at[i], obuf.at[me], loc_sem.at[2])

    def dq_own(i):
        return pltpu.make_async_copy(dqsend.at[i], dqbuf.at[me], loc_sem.at[3])

    @pl.loop(0, 4)
    def _(n):
        i = 3 - n

        @pl.when(i < 3)
        def _():
            z_recv(i)

        from_summary(qbuf, q_r, q_own, i)
        q0 = query(i)
        position = lax.broadcasted_iota(jnp.int32, (ROWS, ROWS), 0).astype(F32)
        peak = jnp.full((1, ROWS), NEGATIVE, F32)
        for j in range(4):
            s = lax.dot_general(docs[i + j, :ROWS], q0, NT, preferred_element_type=F32) * SCALE
            count = docs[i + j, ROWS:].astype(F32)[:1]
            count = jnp.where(4 * z - 3 + i + j >= 0, count, 0.0)
            count = jnp.concatenate([count, count], 1)
            s = jnp.where(position < count, s, NEGATIVE)
            sbuf[i, j] = s
            peak = jnp.maximum(peak, jnp.max(s, axis=0, keepdims=True))
        total = jnp.zeros((1, ROWS), F32)
        for j in range(4):
            e = jnp.exp(sbuf[i, j] - peak)
            sbuf[i, j] = e
            total = total + jnp.sum(e, axis=0, keepdims=True)
        share = 1.0 / total
        out = jnp.zeros((128, ROWS), F32)
        for j in range(4):
            probs = sbuf[i, j] * share
            sbuf[i, j] = probs
            low = probs.astype(BF16)
            pbuf[i, j] = low
            out = out + lax.dot_general(docs[i + j, :ROWS], low, TN, preferred_element_type=F32)
        out = out.T
        osend[i] = jnp.where(
            low_half(HALF), pltpu.roll(out[:HALF], 64, 1), out[HALF:]
        ).astype(BF16)

        @pl.when(me != 4 + i)
        def _():
            o_copy(i).start()

        @pl.when(me == 4 + i)
        def _():
            o_own(i).start()

    def collect(buf, recv, own, start, masked):
        for h in range(8):
            @pl.when(me == h)
            def _():
                own(quad).wait()

            @pl.when(me != h)
            def _():
                remote(buf.at[h], buf.at[h], recv.at[h], recv.at[h], peer(h)).wait_recv()
        for g in range(4):
            a, b = exchange(buf[2 * g].astype(F32), buf[2 * g + 1].astype(F32))
            pair = jnp.concatenate([a, b], 0)
            if masked:
                pair = jnp.where(row_live, pair, 0.0)
            left[:, start + g * 128:start + (g + 1) * 128] = pair.astype(BF16)

    def piece(columns, y, part):
        rows = pl.ds(pl.multiple_of(y * SLICE, SLICE), SLICE)
        part[y] = lax.dot_general(
            left[:, columns], wcat[rows, columns], NT, preferred_element_type=F32
        ).astype(BF16)

    def row_terms(y, part):
        @pl.loop(0, 4)
        def _(j):
            rows = pl.ds(pl.multiple_of(y * SLICE + j * 256, 256), 256)
            value = part[y, :, pl.ds(pl.multiple_of(j * 256, 256), 256)]
            term = value.astype(F32) * (states[:, rows].astype(F32) * gains[:, rows])
            rterm[...] += term[:, :128] + term[:, 128:]

    def rs_copy(n, part, far, into, send, recv):
        src, dst, y = [
            (part.at[y_far, top], far.at[0], y_r),
            (part.at[y_far, bottom], far.at[1], y_l),
            (part.at[y_r, bottom], into.at[0, bottom], y_r),
            (part.at[y_r, top], into.at[0, top], y_r),
            (part.at[y_l, top], into.at[1, top], y_l),
            (part.at[y_l, bottom], into.at[1, bottom], y_l),
        ][n]
        return remote(src, dst, send.at[n], recv.at[n], at_y(y))

    def rs_recv(n, part, far, into, send, recv):
        dst = [
            far.at[0], far.at[1], into.at[0, bottom], into.at[0, top],
            into.at[1, top], into.at[1, bottom],
        ][n]
        remote(dst, dst, send.at[n], recv.at[n], at_y(y_r)).wait_recv()

    def rs_begin(columns, with_rows, args):
        part = args[0]
        piece(columns, y_far, part)
        rs_copy(0, *args).start()
        rs_copy(1, *args).start()
        piece(columns, y_r, part)
        rs_copy(2, *args).start()
        piece(columns, y_l, part)
        rs_copy(4, *args).start()
        piece(columns, mp, part)
        if with_rows:
            for y in (y_far, y_r, y_l, mp):
                row_terms(y, part)

    def rs_middle(args):
        part, far = args[:2]
        rs_recv(0, *args)
        part[y_r, top] = (part[y_r, top].astype(F32) + far[0].astype(F32)).astype(BF16)
        rs_copy(3, *args).start()
        rs_recv(1, *args)
        part[y_l, bottom] = (part[y_l, bottom].astype(F32) + far[1].astype(F32)).astype(BF16)
        rs_copy(5, *args).start()

    def rs_wait(args):
        for n in (2, 4, 3, 5):
            rs_recv(n, *args)

    l_args = (lpart, lfar, lin, l_s, l_r)
    g_args = (gpart, gfar, gin, rs_s, rs_r)
    first, second = pl.ds(0, GROUP), pl.ds(GROUP, GROUP)

    @pl.when(seg == 1)
    def _():
        for n in (1, 3):
            cot_recv(n)

        def gather_product(k):
            c = lax.rem(y_far + k, 4)
            rows = pl.ds(pl.multiple_of(c * SLICE, SLICE), SLICE)
            acc[:, GROUP:] += jnp.dot(cot[c], wcat[rows, GROUP:], preferred_element_type=F32)

        pl.loop(1, 4)(gather_product)
        for n in (4, 5):
            cot_recv(n)
        gather_product(0)

        for g in range(4):
            pair = jnp.where(row_live, acc[:, GROUP + g * 128:GROUP + (g + 1) * 128], 0.0)
            even, odd = exchange(pair[:HALF], pair[HALF:])
            dsend[2 * g] = even.astype(BF16)
            dsend[2 * g + 1] = odd.astype(BF16)
        for k in range(1, 8):
            d_copy(lax.rem(me + k, 8)).start()
        d_own.start()
        collect(obuf, o_r, o_own, GROUP, True)
        rs_begin(second, False, l_args)


    def zg_copy(s):
        return remote(zout.at[s], zin.at[s], zg_s.at[s], zg_r.at[s], at_z(z_dn))

    for i in range(4):
        from_summary(dbuf, d_r, d_own, i)

    for i in range(4):
        q0 = query(i)
        d0 = gradient(i)
        qd = q0 + d0
        delta = jnp.zeros((1, ROWS), F32)
        for j in range(4):
            dp = lax.dot_general(docs[i + j, :ROWS], d0, NT, preferred_element_type=F32)
            dpbuf[i % 2, j] = dp
            delta = delta + jnp.sum(sbuf[i, j] * dp, axis=0, keepdims=True)
        out = jnp.zeros((128, ROWS), F32)
        low = low_half(ROWS)
        for j in range(4):
            ds = (sbuf[i, j] * (dpbuf[i % 2, j] - delta)).astype(BF16)
            out = out + lax.dot_general(docs[i + j, :ROWS], ds, TN, preferred_element_type=F32)
            gk = jnp.dot(ds, qd, preferred_element_type=F32)
            gv = jnp.dot(pbuf[i, j], qd, preferred_element_type=F32)
            gacc[i + j] += jnp.where(low, SCALE * gk, gv)
        out = (SCALE * out).T
        dqsend[i] = jnp.where(
            low_half(HALF), out[:HALF], pltpu.roll(out[HALF:], 64, 1)
        ).astype(BF16)
        if i < 3:
            zout[i] = gacc[i].astype(BF16)
            zg_copy(i).start()

    def g_copy(j):
        return remote(gout.at[j], gbuf.at[me], g_s.at[j], g_r.at[me], peer(j))

    def g_own(j):
        return pltpu.make_async_copy(gout.at[j], gbuf.at[me], loc_sem.at[2])

    for j in range(4):
        if j == 1:
            for i in range(4):
                @pl.when(me != 4 + i)
                def _():
                    dq_copy(i).start()

                @pl.when(me == 4 + i)
                def _():
                    dq_own(i).start()

        total = gacc[3 + j]
        if j > 0:
            remote(zin.at[j - 1], zin.at[j - 1], zg_s.at[0], zg_r.at[j - 1], at_z(z_up)).wait_recv()
            total = total + zin[j - 1].astype(F32)
        gout[j] = total.astype(BF16)

        @pl.when(me != j)
        def _():
            g_copy(j).start()

        @pl.when(me == j)
        def _():
            g_own(j).start()


    @pl.when(seg == 1)
    def _():
        rs_middle(l_args)
        collect(dqbuf, dq_r, dq_own, 0, False)
        rs_begin(first, True, g_args)

    @pl.when(seg == 0)
    def _():
        for h in range(8):
            @pl.when(me == h)
            def _():
                g_own(quad).wait()

            @pl.when(me != h)
            def _():
                remote(gbuf.at[h], gbuf.at[h], g_r.at[h], g_r.at[h], peer(h)).wait_recv()
        for g in range(4):
            a, b = exchange(gbuf[2 * g].astype(F32), gbuf[2 * g + 1].astype(F32))
            left[:, g * 128:(g + 1) * 128] = a.astype(BF16)
            left[:, GROUP + g * 128:GROUP + (g + 1) * 128] = b.astype(BF16)
        rs_begin(pl.ds(0, 2 * GROUP), True, g_args)

    rsend[...] = jnp.broadcast_to(jnp.sum(rterm[...].T, axis=0, keepdims=True), (8, ROWS))

    def rt_copy(n, y):
        return remote(rsend, rin.at[n], rt_s.at[n], rt_r.at[n], at_y(y))

    for n, y in enumerate((y_r, y_l, y_far)):
        rt_copy(n, y).start()

    rs_middle(g_args)

    layer_out = pltpu.make_async_copy(lout, seg_hbm.at[0], out_sem.at[0])

    @pl.when(seg == 1)
    def _():
        rs_wait(l_args)

        @pl.loop(0, 8)
        def _(i):
            rows = pl.ds(pl.multiple_of(i * 32, 32), 32)
            value = lpart[mp, rows].astype(F32) + lin[0, rows].astype(F32) + lin[1, rows].astype(F32)
            lout[rows] = value.astype(BF16)

        layer_out.start()

    for n in range(3):
        remote(rin.at[n], rin.at[n], rt_s.at[n], rt_r.at[n], at_y(y_r)).wait_recv()
    sums = (rsend[...] + rin[0]) + (rin[1] + rin[2])
    rterm[...] = jnp.broadcast_to(sums[:1], (128, ROWS)).T

    rs_wait(g_args)

    @pl.loop(0, 8)
    def _(i):
        rows = pl.ds(pl.multiple_of(i * 32, 32), 32)
        value = gpart[mp, rows].astype(F32) + gin[0, rows].astype(F32) + gin[1, rows].astype(F32)
        inverse = rspread[rows]
        factor = rterm[rows] * (inverse * inverse * inverse) * (1.0 / WIDTH)
        gain = gains[:, own_columns]
        x = states[rows, own_columns].astype(F32)
        gfin[rows] = (gain * value * inverse[:, :1] - x * factor[:, :1]).astype(BF16)

    grad_out = pltpu.make_async_copy(gfin, grad_hbm.at[0], out_sem.at[1])
    grad_out.start()

    @pl.when(seg == 0)
    def _():
        normed_out.wait()
        for k in range(1, 8):
            kv_copy(lax.rem(me + k, 8)).wait_send()

    @pl.when(seg == 1)
    def _():
        layer_out.wait()
        for n in range(6):
            cot_copy(n).wait_send()
            rs_copy(n, *l_args).wait_send()
        for k in range(1, 8):
            q_copy(lax.rem(me + k, 8)).wait_send()
            d_copy(lax.rem(me + k, 8)).wait_send()

    for s in range(3):
        z_copy(s).wait_send()
        zg_copy(s).wait_send()
    for i in range(4):
        @pl.when(me != 4 + i)
        def _():
            o_copy(i).wait_send()
            dq_copy(i).wait_send()

        @pl.when(me != i)
        def _():
            g_copy(i).wait_send()
    for n in range(6):
        rs_copy(n, *g_args).wait_send()
    for n, y in enumerate((y_r, y_l, y_far)):
        rt_copy(n, y).wait_send()
    grad_out.wait()


def deliver(seg_in, grad_in, seg_out, grad_out):
    seg_out[...] = seg_in[...]
    grad_out[...] = grad_in[...]


def per_device(segment_in, norm_gains, projections, live_counts, cotangent):
    dma = lambda n: pltpu.SemaphoreType.DMA((n,))
    vmem = pltpu.VMEM
    shape = jax.ShapeDtypeStruct((1, ROWS, SLICE), BF16)
    hbm = pl.BlockSpec(memory_space=pl.ANY)
    half = pl.BlockSpec((1, HALF, SLICE), lambda i: (0, i, 0))
    results = pl.pallas_call(
        kernel,
        name="window_attention",
        out_shape=(shape, shape),
        in_specs=[pl.BlockSpec(memory_space=pltpu.SMEM)] + [hbm] * 4,
        out_specs=(hbm, hbm),
        scratch_shapes=[
            vmem((ROWS, WIDTH), BF16),
            vmem((1, WIDTH), F32),
            vmem((ROWS, WIDTH), BF16),
            vmem((ROWS, 128), F32),
            vmem((WIDTH, 2, GROUP), BF16),
            vmem((WIDTH, 2 * GROUP), BF16),
            vmem((ROWS, 2 * GROUP), F32),
            vmem((4, ROWS, SLICE), BF16),
            vmem((8, SLAB, 128), BF16),
            vmem((8, HALF, 128), BF16),
            vmem((8, HALF, 128), BF16),
            vmem((7, SLAB, 128), BF16),
            vmem((4, HALF, 128), BF16),
            vmem((4, HALF, 128), BF16),
            vmem((4, 4, ROWS, ROWS), F32),
            vmem((4, 4, ROWS, ROWS), BF16),
            vmem((2, 4, ROWS, ROWS), F32),
            vmem((7, ROWS, 128), F32),
            vmem((4, HALF, 128), BF16),
            vmem((4, HALF, 128), BF16),
            vmem((8, HALF, 128), BF16),
            vmem((8, HALF, 128), BF16),
            vmem((3, ROWS, 128), BF16),
            vmem((3, ROWS, 128), BF16),
            vmem((4, ROWS, 128), BF16),
            vmem((8, ROWS, 128), BF16),
            vmem((ROWS, 2 * GROUP), BF16),
            vmem((4, ROWS, SLICE), BF16),
            vmem((2, HALF, SLICE), BF16),
            vmem((2, ROWS, SLICE), BF16),
            vmem((4, ROWS, SLICE), BF16),
            vmem((2, HALF, SLICE), BF16),
            vmem((2, ROWS, SLICE), BF16),
            vmem((ROWS, 128), F32),
            vmem((8, ROWS), F32),
            vmem((3, 8, ROWS), F32),
            vmem((ROWS, SLICE), BF16),
            vmem((ROWS, SLICE), BF16),
            dma(3), dma(4), dma(4), dma(2),
            dma(6), dma(6), dma(8), dma(7), dma(8), dma(4), dma(8), dma(4), dma(3), dma(3),
            dma(4), dma(8), dma(4), dma(8), dma(3), dma(3), dma(4), dma(8),
            dma(6), dma(6), dma(6), dma(6), dma(3), dma(3),
        ],
        compiler_params=pltpu.CompilerParams(
            collective_id=0, has_side_effects=True, vmem_limit_bytes=56 * 1024 * 1024
        ),
        cost_estimate=pl.CostEstimate(flops=10**10, bytes_accessed=12 * 2**20, transcendentals=2**20),
    )(live_counts.reshape(1, 2), segment_in, norm_gains, projections, cotangent)
    return pl.pallas_call(
        deliver,
        name="deliver",
        out_shape=(shape, shape),
        grid=(2,),
        in_specs=[half] * 2,
        out_specs=(half, half),
    )(*results)


def solution(mesh):
    in_specs = (
        P("segment", "blk", None),
        P("segment", None),
        P("segment", None, None, "mp"),
        P(None, "blk"),
        P("blk", "mp"),
    )
    out_specs = (P("segment", "blk", "mp"), P("segment", "blk", "mp"))
    return jax.shard_map(
        per_device, mesh=mesh, in_specs=in_specs, out_specs=out_specs, check_vma=False
    )
```

```python
import jax
import jax.numpy as jnp
from jax import lax
from jax.experimental import pallas as pl
from jax.experimental.pallas import tpu as pltpu
from jax.sharding import PartitionSpec as P

MESH = pl.DeviceIdType.MESH
F32 = jnp.float32
BF16 = jnp.bfloat16
EPSILON = 1e-06
SCALE = 0.125
NEGATIVE = -1e30
NT = (((1,), (1,)), ((), ()))
TN = (((0,), (0,)), ((), ()))
ROWS = 256
HALF = 128
WIDTH = 4096
SLICE = 1024
GROUP = 512
SLAB = ROWS + 16


def kernel(
    live_ref, x_hbm, gain_hbm, w_hbm, cot_hbm,
    seg_hbm, grad_hbm,
    states, gains, normed, rspread, wraw, wcat, acc, cot,
    kvsend, qsend, dsend, docs, qbuf, dbuf,
    sbuf, pbuf, dpbuf, gacc, osend, dqsend, obuf, dqbuf,
    zout, zin, gout, gbuf,
    left, lpart, lfar, lin, gpart, gfar, gin,
    rterm, rsend, rin, lout, gfin,
    load_sem, w_sem, loc_sem, out_sem,
    cot_s, cot_r, kv_s, doc_r, q_s, q_r, d_s, d_r, z_s, z_r,
    o_s, o_r, dq_s, dq_r, zg_s, zg_r, g_s, g_r,
    l_s, l_r, rs_s, rs_r, rt_s, rt_r,
):
    seg = lax.axis_index("segment")
    blk = lax.axis_index("blk")
    mp = lax.axis_index("mp")
    z = blk // 4
    quad = lax.rem(blk, 4)
    me = seg * 4 + quad
    n_z = lax.axis_size("blk") // 4
    z_up = lax.rem(z + 1, n_z)
    z_dn = lax.rem(z + n_z - 1, n_z)
    y_r, y_l, y_far = lax.rem(mp + 1, 4), lax.rem(mp + 3, 4), lax.rem(mp + 2, 4)

    def peer(t):
        return (t // 4, z * 4 + lax.rem(t, 4), mp)

    def at_y(y):
        return (seg, blk, y)

    def at_z(zz):
        return (seg, zz * 4 + quad, mp)

    def remote(src, dst, send, recv, to):
        return pltpu.make_async_remote_copy(
            src_ref=src, dst_ref=dst, send_sem=send, recv_sem=recv,
            device_id=to, device_id_type=MESH,
        )

    x_load = pltpu.make_async_copy(x_hbm.at[0], states, load_sem.at[0])
    g_load = pltpu.make_async_copy(gain_hbm, gains, load_sem.at[1])
    c_load = pltpu.make_async_copy(cot_hbm, cot.at[mp], load_sem.at[2])
    x_load.start()
    g_load.start()

    @pl.when(seg == 1)
    def _():
        c_load.start()

    def w_load(c):
        rows = pl.ds(pl.multiple_of(c * SLICE, SLICE), SLICE)
        return pltpu.make_async_copy(w_hbm.at[0, rows], wraw.at[rows], w_sem.at[c])

    for c in range(4):
        w_load(c).start()

    barrier = pltpu.get_barrier_semaphore()
    for k in range(1, 8):
        pl.semaphore_signal(barrier, inc=1, device_id=peer(lax.rem(me + k, 8)), device_id_type=MESH)
    for to in (at_y(y_r), at_y(y_l), at_y(y_far), at_z(z_up), at_z(z_dn)):
        pl.semaphore_signal(barrier, inc=1, device_id=to, device_id_type=MESH)

    top, bottom = pl.ds(0, HALF), pl.ds(HALF, HALF)

    def cot_copy(n):
        own_r = lambda h: (cot.at[mp, h], at_y(y_r))
        own_l = lambda h: (cot.at[mp, h], at_y(y_l))
        ref, to = [
            own_r(top), own_r(bottom), own_l(bottom), own_l(top),
            (cot.at[y_l, top], at_y(y_r)), (cot.at[y_r, bottom], at_y(y_l)),
        ][n]
        return remote(ref, ref, cot_s.at[n], cot_r.at[n], to)

    def cot_recv(n):
        ref = [
            cot.at[y_l, top], cot.at[y_l, bottom], cot.at[y_r, bottom], cot.at[y_r, top],
            cot.at[y_far, top], cot.at[y_far, bottom],
        ][n]
        remote(ref, ref, cot_s.at[n], cot_r.at[n], at_y(y_r)).wait_recv()

    def norm(i):
        rows = pl.ds(pl.multiple_of(i * 32, 32), 32)
        x = states[rows].astype(F32)
        inverse = 1.0 / jnp.sqrt(jnp.mean(x * x, axis=-1, keepdims=True) + EPSILON)
        rspread[rows] = jnp.broadcast_to(inverse, (32, 128))
        normed[rows] = (x * inverse * gains[...]).astype(BF16)

    x_load.wait()
    g_load.wait()
    pl.loop(0, 4)(norm)

    @pl.when(seg == 1)
    def _():
        pl.semaphore_wait(barrier, 12)
        c_load.wait()
        for n in (0, 2):
            cot_copy(n).start()

    pl.loop(4, 8)(norm)

    own_columns = pl.ds(pl.multiple_of(mp * SLICE, SLICE), SLICE)
    normed_out = pltpu.make_async_copy(normed.at[:, own_columns], seg_hbm.at[0], out_sem.at[0])

    @pl.when(seg == 0)
    def _():
        normed_out.start()

    def low_half(rows):
        return lax.broadcasted_iota(jnp.int32, (rows, 128), 1) < 64

    def exchange(a, b):
        low = low_half(a.shape[0])
        return jnp.where(low, a, pltpu.roll(b, 64, 1)), jnp.where(low, pltpu.roll(a, 64, 1), b)

    row_live = lax.broadcasted_iota(jnp.int32, (ROWS, 128), 0) < live_ref[0, 1]

    def kv_copy(t):
        return remote(kvsend.at[t], docs.at[3 + quad], kv_s.at[t], doc_r.at[3 + quad], peer(t))

    def q_copy(t):
        return remote(qsend.at[t], qbuf.at[quad], q_s.at[t], q_r.at[quad], peer(t))

    def d_copy(t):
        return remote(dsend.at[t], dbuf.at[quad], d_s.at[t], d_r.at[quad], peer(t))

    kv_own = pltpu.make_async_copy(kvsend.at[me], docs.at[3 + quad], loc_sem.at[0])
    q_own = pltpu.make_async_copy(qsend.at[me], qbuf.at[quad], loc_sem.at[0])
    d_own = pltpu.make_async_copy(dsend.at[me], dbuf.at[quad], loc_sem.at[1])

    def spread_weights(c):
        w_load(c).wait()

        @pl.loop(0, 4)
        def _(j):
            rows = pl.ds(pl.multiple_of(c * SLICE + j * 256, 256), 256)
            wcat[rows] = wraw[rows].reshape(256, 2 * GROUP)

    @pl.when(seg == 0)
    def _():
        pl.loop(0, 4)(spread_weights)
        pl.semaphore_wait(barrier, 12)
        count = jnp.full((16, 128), live_ref[0, 0], jnp.int32).astype(F32).astype(BF16)
        for stage in (1, 0):
            start = stage * 256
            keys = jnp.dot(normed[...], wcat[:, start:start + 256], preferred_element_type=F32)
            start = GROUP + start
            values = jnp.dot(normed[...], wcat[:, start:start + 256], preferred_element_type=F32)
            for g in range(2):
                part = slice(g * 128, (g + 1) * 128)
                for k, slab in enumerate(exchange(keys[:, part], values[:, part])):
                    t = 4 * stage + 2 * g + k
                    kvsend[t, :ROWS] = slab.astype(BF16)
                    kvsend[t, ROWS:] = count
            for k in range(4):
                t = 4 * stage + lax.rem(quad + k, 4)
                if stage == 0 and k == 0:
                    kv_own.start()
                else:
                    kv_copy(t).start()

    @pl.when(seg == 1)
    def _():
        acc[...] = jnp.zeros_like(acc)

        @pl.loop(0, 4)
        def _(c):
            spread_weights(c)
            rows = pl.ds(pl.multiple_of(c * SLICE, SLICE), SLICE)
            acc[:, :GROUP] += jnp.dot(
                normed[:, rows], wcat[rows, :GROUP], preferred_element_type=F32
            )

        for g in range(4):
            pair = acc[:, g * 128:(g + 1) * 128]
            even, odd = exchange(pair[:HALF], pair[HALF:])
            qsend[2 * g] = even.astype(BF16)
            qsend[2 * g + 1] = odd.astype(BF16)
        for k in range(1, 8):
            q_copy(lax.rem(me + k, 8)).start()
        q_own.start()
        cot_recv(0)
        cot_recv(2)
        for n in (1, 3, 4, 5):
            cot_copy(n).start()

    def z_copy(s):
        return remote(docs.at[s + 4], docs.at[s], z_s.at[s], z_r.at[s], at_z(z_up))

    def z_recv(s):
        remote(docs.at[s], docs.at[s], z_s.at[s], z_r.at[s], at_z(z_up)).wait_recv()

    for j in (3, 2, 1, 0):
        @pl.when(me == j)
        def _():
            kv_own.wait()

        @pl.when(me != j)
        def _():
            remote(docs.at[3 + j], docs.at[3 + j], kv_s.at[0], doc_r.at[3 + j], peer(j)).wait_recv()

        if j > 0:
            z_copy(j - 1).start()

    def from_summary(buf, recv, own, i):
        @pl.when(me == 4 + i)
        def _():
            own.wait()

        @pl.when(me != 4 + i)
        def _():
            remote(buf.at[i], buf.at[i], recv.at[i], recv.at[i], peer(4 + i)).wait_recv()

    def query(i):
        slab = qbuf[i].astype(F32)
        low = low_half(HALF)
        a = jnp.where(low, slab, 0.0)
        b = jnp.where(low, pltpu.roll(slab, 64, 1), 0.0)
        return jnp.concatenate([a, b], 0).astype(BF16)

    def gradient(i):
        slab = dbuf[i].astype(F32)
        low = low_half(HALF)
        a = jnp.where(low, 0.0, pltpu.roll(slab, 64, 1))
        b = jnp.where(low, 0.0, slab)
        return jnp.concatenate([a, b], 0).astype(BF16)

    def o_copy(i):
        return remote(osend.at[i], obuf.at[me], o_s.at[i], o_r.at[me], peer(4 + i))

    def dq_copy(i):
        return remote(dqsend.at[i], dqbuf.at[me], dq_s.at[i], dq_r.at[me], peer(4 + i))

    def o_own(i):
        return pltpu.make_async_copy(osend.at[i], obuf.at[me], loc_sem.at[2])

    def dq_own(i):
        return pltpu.make_async_copy(dqsend.at[i], dqbuf.at[me], loc_sem.at[3])

    @pl.loop(0, 4)
    def _(n):
        i = 3 - n

        @pl.when(i < 3)
        def _():
            z_recv(i)

        from_summary(qbuf, q_r, q_own, i)
        q0 = query(i)
        position = lax.broadcasted_iota(jnp.int32, (ROWS, ROWS), 0).astype(F32)
        peak = jnp.full((1, ROWS), NEGATIVE, F32)
        for j in range(4):
            s = lax.dot_general(docs[i + j, :ROWS], q0, NT, preferred_element_type=F32) * SCALE
            count = docs[i + j, ROWS:].astype(F32)[:1]
            count = jnp.where(4 * z - 3 + i + j >= 0, count, 0.0)
            count = jnp.concatenate([count, count], 1)
            s = jnp.where(position < count, s, NEGATIVE)
            sbuf[i, j] = s
            peak = jnp.maximum(peak, jnp.max(s, axis=0, keepdims=True))
        total = jnp.zeros((1, ROWS), F32)
        for j in range(4):
            e = jnp.exp(sbuf[i, j] - peak)
            sbuf[i, j] = e
            total = total + jnp.sum(e, axis=0, keepdims=True)
        share = 1.0 / total
        out = jnp.zeros((128, ROWS), F32)
        for j in range(4):
            probs = sbuf[i, j] * share
            sbuf[i, j] = probs
            low = probs.astype(BF16)
            pbuf[i, j] = low
            out = out + lax.dot_general(docs[i + j, :ROWS], low, TN, preferred_element_type=F32)
        out = out.T
        osend[i] = jnp.where(
            low_half(HALF), pltpu.roll(out[:HALF], 64, 1), out[HALF:]
        ).astype(BF16)

        @pl.when(me != 4 + i)
        def _():
            o_copy(i).start()

        @pl.when(me == 4 + i)
        def _():
            o_own(i).start()

    def collect(buf, recv, own, start, masked):
        for h in range(8):
            @pl.when(me == h)
            def _():
                own(quad).wait()

            @pl.when(me != h)
            def _():
                remote(buf.at[h], buf.at[h], recv.at[h], recv.at[h], peer(h)).wait_recv()
        for g in range(4):
            a, b = exchange(buf[2 * g].astype(F32), buf[2 * g + 1].astype(F32))
            pair = jnp.concatenate([a, b], 0)
            if masked:
                pair = jnp.where(row_live, pair, 0.0)
            left[:, start + g * 128:start + (g + 1) * 128] = pair.astype(BF16)

    def piece(columns, y, part):
        rows = pl.ds(pl.multiple_of(y * SLICE, SLICE), SLICE)
        part[y] = lax.dot_general(
            left[:, columns], wcat[rows, columns], NT, preferred_element_type=F32
        ).astype(BF16)

    def row_terms(y, part):
        @pl.loop(0, 4)
        def _(j):
            rows = pl.ds(pl.multiple_of(y * SLICE + j * 256, 256), 256)
            value = part[y, :, pl.ds(pl.multiple_of(j * 256, 256), 256)]
            term = value.astype(F32) * (states[:, rows].astype(F32) * gains[:, rows])
            rterm[...] += term[:, :128] + term[:, 128:]

    quarters = [pl.ds(n * 64, 64) for n in range(4)]

    def rs_copy(n, part, far, into, send, recv):
        src, dst, y = (
            [(part.at[y_far, r], far.at[r], y_r) for r in quarters[:2]]
            + [(part.at[y_far, r], far.at[r], y_l) for r in quarters[2:]]
            + [(part.at[y_r, bottom], into.at[0, bottom], y_r)]
            + [(part.at[y_l, top], into.at[1, top], y_l)]
            + [(part.at[y_r, r], into.at[0, r], y_r) for r in quarters[:2]]
            + [(part.at[y_l, r], into.at[1, r], y_l) for r in quarters[2:]]
        )[n]
        return remote(src, dst, send.at[n], recv.at[n], at_y(y))

    def rs_recv(n, part, far, into, send, recv):
        dst = (
            [far.at[r] for r in quarters]
            + [into.at[0, bottom], into.at[1, top]]
            + [into.at[0, r] for r in quarters[:2]]
            + [into.at[1, r] for r in quarters[2:]]
        )[n]
        remote(dst, dst, send.at[n], recv.at[n], at_y(y_r)).wait_recv()

    def rs_begin(columns, with_rows, args):
        part = args[0]
        piece(columns, y_far, part)
        for n in (0, 2, 1, 3):
            rs_copy(n, *args).start()
        piece(columns, y_r, part)
        rs_copy(4, *args).start()
        piece(columns, y_l, part)
        rs_copy(5, *args).start()
        piece(columns, mp, part)
        if with_rows:
            for y in (y_far, y_r, y_l, mp):
                row_terms(y, part)

    def rs_middle(args):
        part, far = args[:2]
        for n, y in ((0, y_r), (2, y_l), (1, y_r), (3, y_l)):
            rs_recv(n, *args)
            rows = quarters[n]
            part[y, rows] = (part[y, rows].astype(F32) + far[rows].astype(F32)).astype(BF16)
            rs_copy(6 + n, *args).start()

    def rs_wait(args):
        for n in range(4, 10):
            rs_recv(n, *args)

    l_args = (lpart, lfar, lin, l_s, l_r)
    g_args = (gpart, gfar, gin, rs_s, rs_r)
    first, second = pl.ds(0, GROUP), pl.ds(GROUP, GROUP)

    @pl.when(seg == 1)
    def _():
        for n in (1, 3):
            cot_recv(n)

        def gather_product(k):
            c = lax.rem(y_far + k, 4)
            rows = pl.ds(pl.multiple_of(c * SLICE, SLICE), SLICE)
            acc[:, GROUP:] += jnp.dot(cot[c], wcat[rows, GROUP:], preferred_element_type=F32)

        pl.loop(1, 4)(gather_product)
        for n in (4, 5):
            cot_recv(n)
        gather_product(0)

        for g in range(4):
            pair = jnp.where(row_live, acc[:, GROUP + g * 128:GROUP + (g + 1) * 128], 0.0)
            even, odd = exchange(pair[:HALF], pair[HALF:])
            dsend[2 * g] = even.astype(BF16)
            dsend[2 * g + 1] = odd.astype(BF16)
        for k in range(1, 8):
            d_copy(lax.rem(me + k, 8)).start()
        d_own.start()
        collect(obuf, o_r, o_own, GROUP, True)
        rs_begin(second, False, l_args)

    gacc[...] = jnp.zeros_like(gacc)

    def zg_copy(s):
        return remote(zout.at[s], zin.at[s], zg_s.at[s], zg_r.at[s], at_z(z_dn))

    for i in range(4):
        from_summary(dbuf, d_r, d_own, i)

    for i in range(4):
        q0 = query(i)
        d0 = gradient(i)
        qd = q0 + d0
        delta = jnp.zeros((1, ROWS), F32)
        for j in range(4):
            dp = lax.dot_general(docs[i + j, :ROWS], d0, NT, preferred_element_type=F32)
            dpbuf[i % 2, j] = dp
            delta = delta + jnp.sum(sbuf[i, j] * dp, axis=0, keepdims=True)
        out = jnp.zeros((128, ROWS), F32)
        low = low_half(ROWS)
        for j in range(4):
            ds = (sbuf[i, j] * (dpbuf[i % 2, j] - delta)).astype(BF16)
            out = out + lax.dot_general(docs[i + j, :ROWS], ds, TN, preferred_element_type=F32)
            gk = jnp.dot(ds, qd, preferred_element_type=F32)
            gv = jnp.dot(pbuf[i, j], qd, preferred_element_type=F32)
            gacc[i + j] += jnp.where(low, SCALE * gk, gv)
        out = (SCALE * out).T
        dqsend[i] = jnp.where(
            low_half(HALF), out[:HALF], pltpu.roll(out[HALF:], 64, 1)
        ).astype(BF16)
        if i < 3:
            zout[i] = gacc[i].astype(BF16)
            zg_copy(i).start()

    for i in range(4):
        @pl.when(me != 4 + i)
        def _():
            dq_copy(i).start()

        @pl.when(me == 4 + i)
        def _():
            dq_own(i).start()

    def g_copy(j):
        return remote(gout.at[j], gbuf.at[me], g_s.at[j], g_r.at[me], peer(j))

    def g_own(j):
        return pltpu.make_async_copy(gout.at[j], gbuf.at[me], loc_sem.at[2])

    for j in range(4):
        total = gacc[3 + j]
        if j > 0:
            remote(zin.at[j - 1], zin.at[j - 1], zg_s.at[0], zg_r.at[j - 1], at_z(z_up)).wait_recv()
            total = total + zin[j - 1].astype(F32)
        gout[j] = total.astype(BF16)

        @pl.when(me != j)
        def _():
            g_copy(j).start()

        @pl.when(me == j)
        def _():
            g_own(j).start()

    rterm[...] = jnp.zeros_like(rterm)

    @pl.when(seg == 1)
    def _():
        rs_middle(l_args)
        collect(dqbuf, dq_r, dq_own, 0, False)
        rs_begin(first, True, g_args)

    @pl.when(seg == 0)
    def _():
        for h in range(8):
            @pl.when(me == h)
            def _():
                g_own(quad).wait()

            @pl.when(me != h)
            def _():
                remote(gbuf.at[h], gbuf.at[h], g_r.at[h], g_r.at[h], peer(h)).wait_recv()
        for g in range(4):
            a, b = exchange(gbuf[2 * g].astype(F32), gbuf[2 * g + 1].astype(F32))
            left[:, g * 128:(g + 1) * 128] = a.astype(BF16)
            left[:, GROUP + g * 128:GROUP + (g + 1) * 128] = b.astype(BF16)
        rs_begin(pl.ds(0, 2 * GROUP), True, g_args)

    rsend[...] = jnp.broadcast_to(jnp.sum(rterm[...].T, axis=0, keepdims=True), (8, ROWS))

    def rt_copy(n, y):
        return remote(rsend, rin.at[n], rt_s.at[n], rt_r.at[n], at_y(y))

    for n, y in enumerate((y_r, y_l, y_far)):
        rt_copy(n, y).start()

    rs_middle(g_args)

    layer_out = pltpu.make_async_copy(lout, seg_hbm.at[0], out_sem.at[0])

    @pl.when(seg == 1)
    def _():
        rs_wait(l_args)

        @pl.loop(0, 8)
        def _(i):
            rows = pl.ds(pl.multiple_of(i * 32, 32), 32)
            value = lpart[mp, rows].astype(F32) + lin[0, rows].astype(F32) + lin[1, rows].astype(F32)
            lout[rows] = value.astype(BF16)

        layer_out.start()

    for n in range(3):
        remote(rin.at[n], rin.at[n], rt_s.at[n], rt_r.at[n], at_y(y_r)).wait_recv()
    sums = (rsend[...] + rin[0]) + (rin[1] + rin[2])
    rterm[...] = jnp.broadcast_to(sums[:1], (128, ROWS)).T

    rs_wait(g_args)

    @pl.loop(0, 8)
    def _(i):
        rows = pl.ds(pl.multiple_of(i * 32, 32), 32)
        value = gpart[mp, rows].astype(F32) + gin[0, rows].astype(F32) + gin[1, rows].astype(F32)
        inverse = rspread[rows]
        factor = rterm[rows] * (inverse * inverse * inverse) * (1.0 / WIDTH)
        gain = gains[:, own_columns]
        x = states[rows, own_columns].astype(F32)
        gfin[rows] = (gain * value * inverse[:, :1] - x * factor[:, :1]).astype(BF16)

    grad_out = pltpu.make_async_copy(gfin, grad_hbm.at[0], out_sem.at[1])
    grad_out.start()

    @pl.when(seg == 0)
    def _():
        normed_out.wait()
        for k in range(1, 8):
            kv_copy(lax.rem(me + k, 8)).wait_send()

    @pl.when(seg == 1)
    def _():
        layer_out.wait()
        for n in range(6):
            cot_copy(n).wait_send()
        for n in range(10):
            rs_copy(n, *l_args).wait_send()
        for k in range(1, 8):
            q_copy(lax.rem(me + k, 8)).wait_send()
            d_copy(lax.rem(me + k, 8)).wait_send()

    for s in range(3):
        z_copy(s).wait_send()
        zg_copy(s).wait_send()
    for i in range(4):
        @pl.when(me != 4 + i)
        def _():
            o_copy(i).wait_send()
            dq_copy(i).wait_send()

        @pl.when(me != i)
        def _():
            g_copy(i).wait_send()
    for n in range(10):
        rs_copy(n, *g_args).wait_send()
    for n, y in enumerate((y_r, y_l, y_far)):
        rt_copy(n, y).wait_send()
    grad_out.wait()


def deliver(seg_in, grad_in, seg_out, grad_out):
    seg_out[...] = seg_in[...]
    grad_out[...] = grad_in[...]


def per_device(segment_in, norm_gains, projections, live_counts, cotangent):
    dma = lambda n: pltpu.SemaphoreType.DMA((n,))
    vmem = pltpu.VMEM
    shape = jax.ShapeDtypeStruct((1, ROWS, SLICE), BF16)
    hbm = pl.BlockSpec(memory_space=pl.ANY)
    half = pl.BlockSpec((1, HALF, SLICE), lambda i: (0, i, 0))
    results = pl.pallas_call(
        kernel,
        name="window_attention",
        out_shape=(shape, shape),
        in_specs=[pl.BlockSpec(memory_space=pltpu.SMEM)] + [hbm] * 4,
        out_specs=(hbm, hbm),
        scratch_shapes=[
            vmem((ROWS, WIDTH), BF16),
            vmem((1, WIDTH), F32),
            vmem((ROWS, WIDTH), BF16),
            vmem((ROWS, 128), F32),
            vmem((WIDTH, 2, GROUP), BF16),
            vmem((WIDTH, 2 * GROUP), BF16),
            vmem((ROWS, 2 * GROUP), F32),
            vmem((4, ROWS, SLICE), BF16),
            vmem((8, SLAB, 128), BF16),
            vmem((8, HALF, 128), BF16),
            vmem((8, HALF, 128), BF16),
            vmem((7, SLAB, 128), BF16),
            vmem((4, HALF, 128), BF16),
            vmem((4, HALF, 128), BF16),
            vmem((4, 4, ROWS, ROWS), F32),
            vmem((4, 4, ROWS, ROWS), BF16),
            vmem((2, 4, ROWS, ROWS), F32),
            vmem((7, ROWS, 128), F32),
            vmem((4, HALF, 128), BF16),
            vmem((4, HALF, 128), BF16),
            vmem((8, HALF, 128), BF16),
            vmem((8, HALF, 128), BF16),
            vmem((3, ROWS, 128), BF16),
            vmem((3, ROWS, 128), BF16),
            vmem((4, ROWS, 128), BF16),
            vmem((8, ROWS, 128), BF16),
            vmem((ROWS, 2 * GROUP), BF16),
            vmem((4, ROWS, SLICE), BF16),
            vmem((ROWS, SLICE), BF16),
            vmem((2, ROWS, SLICE), BF16),
            vmem((4, ROWS, SLICE), BF16),
            vmem((ROWS, SLICE), BF16),
            vmem((2, ROWS, SLICE), BF16),
            vmem((ROWS, 128), F32),
            vmem((8, ROWS), F32),
            vmem((3, 8, ROWS), F32),
            vmem((ROWS, SLICE), BF16),
            vmem((ROWS, SLICE), BF16),
            dma(3), dma(4), dma(4), dma(2),
            dma(6), dma(6), dma(8), dma(7), dma(8), dma(4), dma(8), dma(4), dma(3), dma(3),
            dma(4), dma(8), dma(4), dma(8), dma(3), dma(3), dma(4), dma(8),
            dma(10), dma(10), dma(10), dma(10), dma(3), dma(3),
        ],
        compiler_params=pltpu.CompilerParams(
            collective_id=0, has_side_effects=True, vmem_limit_bytes=56 * 1024 * 1024
        ),
        cost_estimate=pl.CostEstimate(flops=10**10, bytes_accessed=12 * 2**20, transcendentals=2**20),
    )(live_counts.reshape(1, 2), segment_in, norm_gains, projections, cotangent)
    return pl.pallas_call(
        deliver,
        name="deliver",
        out_shape=(shape, shape),
        grid=(2,),
        in_specs=[half] * 2,
        out_specs=(half, half),
    )(*results)


def solution(mesh):
    in_specs = (
        P("segment", "blk", None),
        P("segment", None),
        P("segment", None, None, "mp"),
        P(None, "blk"),
        P("blk", "mp"),
    )
    out_specs = (P("segment", "blk", "mp"), P("segment", "blk", "mp"))
    return jax.shard_map(
        per_device, mesh=mesh, in_specs=in_specs, out_specs=out_specs, check_vma=False
    )
```
